32 devices in a mesh: groups: 2 (over y), gx: 16 (over z, x, core).
Axes of the slice: x: 2, y: 2, z: 4, core: 2. Of those that a mesh axis runs over, the one named last changes fastest.
Arguments:
- state: float32 [3, 32, 128, 256], P(None, ('groups', 'gx')), parts along dimension 1, may hold values from -4 to 4
- old_state: float32 [3, 32, 128, 256], P(None, ('groups', 'gx')), parts along dimension 1, may hold values from -4 to 4
- pore_volume: float32 [32, 128, 256], P(('groups', 'gx')), parts along dimension 0, may hold values from 0.5 to 2
- permeability: float32 [32, 128, 256], P(('groups', 'gx')), parts along dimension 0, may hold values from 0.2 to 2
- inverse_blocks: float32 [3, 3, 32, 128, 256], P(None, None, ('groups', 'gx')), parts along dimension 2, may hold values from -0.4 to 0.4
- perf_cells: int32 [2, 512], P(None, ('groups', 'gx')), parts along dimension 1, may hold values from -1 to 32767, as said below
- perf_wells: int32 [2, 512], P(None, ('groups', 'gx')), parts along dimension 1, may hold values from -1 to 15, as said below
- well_index: float32 [2, 512], P(None, ('groups', 'gx')), parts along dimension 1, may hold values from 0.5 to 2
- well_rates: float32 [512], P(('groups', 'gx')), parts along dimension 0, may hold values from -8 to 8
Outputs:
- new_state: float32 [3, 32, 128, 256], P(None, ('groups', 'gx')), parts along dimension 1
- residual: float32 [3, 32, 128, 256], P(None, ('groups', 'gx')), parts along dimension 1
- bottomhole: float32 [512], P(('groups', 'gx')), parts along dimension 0
The draws below stay inside these ranges and needn't reach their ends.
There are 2 independent parts, one for each index of `groups`. The reference program is written for one: setup_inputs(seed, part) draws one part's arguments, and reference() takes and returns one part's arrays. A program takes and returns all parts, laid end to end along the dimension named above; each array names one. Nothing has to cross between parts.
Inputs may be any that keep to these rules, and one draw needn't show every extreme that they name: `perf_cells`: column s * 16 + d, row k: the cell that slot k from device s to owner d perforates, as a row-major index into device s's own cells, or -1 if the slot is empty. Every device fills all its slots to itself, and some device receives all slots filled from every device. `perf_wells`: column d * 16 + s, row k: the well of device d that slot k from device s belongs to, -1 exactly where the matching entry of perf_cells is -1. Every well has at least one live slot.
All inputs are finite; a program needn't handle non-finite values.
Results may differ from the reference program's by a relative error of at most 0.0003.
Values sent between devices are 32-bit elements; how exact they have to be, the bound alone decides.
A program may use at most 128 MiB of HBM per device.

```python
import math
import jax
import jax.numpy as jnp

CX = 1
NY = 128
NZ = 256
WELL_DEV = 16
CAP = 2
SWEEPS = 2
OWNERS = 16
NX = 16
WELLS = 256
PAIRS = 256


def perf_tables(key):
    owners = OWNERS
    keys = jax.random.split(key, 6)
    level = jax.random.randint(keys[0], (owners,), 2, 8)
    busiest = jax.random.randint(keys[1], (), 0, owners)
    level = jnp.where(jnp.arange(owners) == busiest, 10, level)
    roll = jax.random.randint(keys[2], (CAP, owners, owners), 0, 10)
    sender = jnp.arange(owners)[None, :, None]
    target = jnp.arange(owners)[None, None, :]
    slot = jnp.arange(CAP)[:, None, None]
    filled = roll < level[None, None, :]
    offset = jax.random.randint(keys[3], (owners,), 0, owners)
    spacing = (sender - target - offset[None, None, :]) % owners
    cover = (spacing < WELL_DEV) & (slot == 0)
    filled = filled | cover | (sender == target)
    picks = jax.random.randint(keys[4], (3, CAP, owners, owners), 0, WELL_DEV)
    chosen = jnp.min(picks, axis=0)
    chosen = jnp.where(cover, spacing, chosen)
    located = jax.random.randint(keys[5], (CAP, owners, owners), 0, CX * NY * NZ)
    corner = (slot == 0) & (sender == 0) & (target == 0)
    located = jnp.where(corner, CX * NY * NZ - 1, located)
    cells_tab = jnp.where(filled, located, -1).reshape(CAP, owners * owners).astype(jnp.int32)
    wells_tab = jnp.transpose(jnp.where(filled, chosen, -1), (0, 2, 1)).reshape(CAP, owners * owners).astype(jnp.int32)
    return (cells_tab, wells_tab)


def draw_perf_cells(key, part):
    return perf_tables(key)[0]


def draw_perf_wells(key, part):
    return perf_tables(key)[1]


def shard_levels(rng, extent, pieces, least, high):
    gain, own = 1.0, jax.random.fold_in(rng, 6)
    for dim, shards_of in pieces:
        draws = jnp.exp(jax.random.uniform(jax.random.fold_in(own, dim), (shards_of,), jnp.float32, least / len(pieces), high / len(pieces)))
        gain = gain * jnp.repeat(draws, extent[dim] // shards_of).reshape([-1 if axis == dim else 1 for axis in range(len(extent))])
    return gain


def bell_draw(own_key, extent, spread, reach, pieces=(), held_as=jnp.bfloat16):
    values = spread * jax.random.normal(own_key, extent, jnp.float32)
    if pieces:
        values = values * shard_levels(own_key, extent, pieces, -0.22, 0.18)
    return jnp.clip(values, -reach, reach).astype(held_as)


def setup_inputs(seed: int = 0, part: int = 0) -> dict:
    key_list = jax.random.split(jax.random.key(seed), 10)
    own_keys = jax.random.split(jax.random.fold_in(key_list[9], part), 10)
    state = bell_draw(own_keys[0], (3, NX, NY, NZ), 1.0, 4.0, ((1, 16),), jnp.float32)
    old_state = bell_draw(own_keys[1], (3, NX, NY, NZ), 1.0, 4.0, ((1, 16),), jnp.float32)
    pore_volume = jnp.clip(jnp.exp(math.log(2.0) - 1.3862944 * jax.random.uniform(own_keys[2], (NX, NY, NZ), jnp.float32) ** shard_levels(own_keys[2], (NX, NY, NZ), ((0, 16),), -0.2, 0.2)), 0.5, 2.0)
    permeability = jnp.clip(jnp.exp(math.log(2.0) - 2.3025851 * jax.random.uniform(own_keys[3], (NX, NY, NZ), jnp.float32) ** shard_levels(own_keys[3], (NX, NY, NZ), ((0, 16),), -0.2, 0.2)), 0.2, 2.0)
    inverse_blocks = bell_draw(own_keys[4], (3, 3, NX, NY, NZ), 0.08, 0.4, ((2, 16),), jnp.float32)
    perf_cells = draw_perf_cells(jax.random.fold_in(jax.random.fold_in(key_list[9], part), 71), part)
    perf_wells = draw_perf_wells(jax.random.fold_in(jax.random.fold_in(key_list[9], part), 71), part)
    well_index = jnp.clip(jnp.exp(math.log(2.0) - 1.3862944 * jax.random.uniform(own_keys[7], (CAP, PAIRS), jnp.float32) ** shard_levels(own_keys[7], (CAP, PAIRS), ((1, 16),), -0.2, 0.2)), 0.5, 2.0)
    well_rates = bell_draw(own_keys[8], (WELLS,), 2.0, 8.0, ((0, 16),), jnp.float32)
    return dict(state=state, old_state=old_state, pore_volume=pore_volume, permeability=permeability, inverse_blocks=inverse_blocks, perf_cells=perf_cells, perf_wells=perf_wells, well_index=well_index, well_rates=well_rates)


def fractions(unknowns):
    first = jnp.exp(jnp.tanh(unknowns[1]))
    second = jnp.exp(jnp.tanh(unknowns[2]))
    total = 1.0 + first + second
    return jnp.stack([1.0 / total, first / total, second / total])


def accumulate(values):
    return values + 0.5 * jnp.tanh(values)


def shifted(array, step_x, step_y, step_z):
    size_x, size_y, size_z = array.shape[-3], array.shape[-2], array.shape[-1]
    return array[..., 1 + step_x:size_x - 1 + step_x, 1 + step_y:size_y - 1 + step_y, 1 + step_z:size_z - 1 + step_z]


def flux_sum(ext_u, ext_k):
    frac = fractions(ext_u)
    press = ext_u[0]
    k_center = shifted(ext_k, 0, 0, 0)
    p_center = shifted(press, 0, 0, 0)
    f_center = shifted(frac, 0, 0, 0)
    total = jnp.zeros_like(f_center)
    for step_x, step_y, step_z in ((1, 0, 0), (-1, 0, 0), (0, 1, 0), (0, -1, 0), (0, 0, 1), (0, 0, -1)):
        k_near = shifted(ext_k, step_x, step_y, step_z)
        p_near = shifted(press, step_x, step_y, step_z)
        f_near = shifted(frac, step_x, step_y, step_z)
        trans = 2.0 * k_center * k_near / (k_center + k_near)
        total = total + (trans * (p_center - p_near))[None] * 0.5 * (f_center + f_near)
    return total


def cell_part(ext_u, ext_k, pore, old):
    center = ext_u[:, 1:-1, 1:-1, 1:-1]
    return pore[None] * (accumulate(center) - accumulate(old)) + flux_sum(ext_u, ext_k)


def owner(blocks, wells, index_w, rates):
    valid = wells >= 0
    weight = jnp.where(valid, index_w, 0.0)
    count = rates.shape[0]
    onehot = (wells[None] == jnp.arange(count, dtype=jnp.int32)[:, None, None]).astype(rates.dtype)
    weight_sum = jnp.sum(onehot * weight[None], axis=(1, 2))
    press_sum = jnp.sum(onehot * (weight * blocks[0])[None], axis=(1, 2))
    bottom = (rates + press_sum) / weight_sum
    at_slot = jnp.sum(onehot * bottom[:, None, None], axis=0)
    flow = weight * (at_slot - blocks[0])
    return flow[None] * fractions(blocks), bottom


def apply_blocks(blocks, values):
    return jnp.sum(blocks * values[None], axis=1)


def reference(state, old_state, pore_volume, permeability, inverse_blocks, perf_cells, perf_wells, well_index, well_rates):
    owners = OWNERS
    cells = CX * NY * NZ
    pad_k = jnp.pad(permeability, 1)
    sender = jnp.arange(owners, dtype=jnp.int32)[None, :, None]
    table = perf_cells.reshape(CAP, owners, owners)
    safe = jnp.maximum(table, 0).astype(jnp.int32)
    mask = (table >= 0).astype(state.dtype)
    wells = perf_wells.reshape(CAP, owners, owners)
    index_w = well_index.reshape(CAP, owners, owners)
    rates = well_rates.reshape(owners, WELL_DEV)

    def residual_fn(current):
        ext_u = jnp.pad(current, ((0, 0), (1, 1), (1, 1), (1, 1)))
        cell = cell_part(ext_u, pad_k, pore_volume, old_state)
        flat = current.reshape(3, owners, cells)
        blocks = flat[:, sender, safe]
        owned = jnp.transpose(blocks, (0, 1, 3, 2))
        sources, bottom = jax.vmap(owner, in_axes=(2, 1, 1, 0), out_axes=(2, 0))(owned, wells, index_w, rates)
        back = jnp.transpose(sources, (0, 1, 3, 2)) * mask[None]
        well_term = jnp.zeros((3, owners, cells), current.dtype).at[:, sender, safe].add(back)
        return cell - well_term.reshape(current.shape), bottom.reshape(-1)

    residual, bottomhole = residual_fn(state)
    correction = jnp.zeros_like(state)
    for sweep in range(SWEEPS):
        if sweep == 0:
            target = -residual
        else:
            tangent = jax.jvp(residual_fn, (state,), (correction,))[1][0]
            target = -residual - tangent
        correction = correction + apply_blocks(inverse_blocks, target)
    return state + correction, residual, bottomhole
```

```python
import functools

import jax
import jax.numpy as jnp
from jax import lax
from jax.experimental import pallas as pl
from jax.experimental.pallas import tpu as pltpu
from jax.sharding import PartitionSpec as P

CHUNKS = 4
MESH = pl.DeviceIdType.MESH
EXACT = lax.Precision.HIGHEST


def contract(left, right, left_dim, right_dim):
    return lax.dot_general(
        left,
        right,
        (((left_dim,), (right_dim,)), ((), ())),
        precision=EXACT,
        preferred_element_type=jnp.float32,
    )


def fractions(first, second):
    e1 = jnp.exp(jnp.tanh(first))
    e2 = jnp.exp(jnp.tanh(second))
    inverse = 1.0 / (1.0 + e1 + e2)
    return e1 * inverse, e2 * inverse


def transmissibility(k_a, k_b):
    return 2.0 * k_a * k_b / (k_a + k_b)


def kernel(
    n,
    state_hbm,
    old_hbm,
    pore_hbm,
    perm_hbm,
    inv_hbm,
    cells_ref,
    wells_ref,
    index_ref,
    rates_ref,
    new_ref,
    res_ref,
    bottom_ref,
    u,
    old,
    pore,
    perm,
    inv,
    halo_u,
    halo_k,
    halo_d,
    send_d,
    corr,
    frac,
    slope,
    accum,
    face,
    edge,
    part,
    source,
    message,
    inbox,
    message_d,
    inbox_d,
    load_sem,
    well_send,
    well_recv,
    welld_send,
    welld_recv,
    bulk_send,
    bulk_recv,
    bulkd_send,
    bulkd_recv,
):
    me = lax.axis_index("gx")
    ny, nz = perm.shape
    rows = ny // CHUNKS
    caps = cells_ref.shape[0]
    nwell = rates_ref.shape[1]

    loads = [
        pltpu.make_async_copy(state_hbm.at[:, 0], u, load_sem.at[0]),
        pltpu.make_async_copy(perm_hbm.at[0], perm, load_sem.at[1]),
        pltpu.make_async_copy(old_hbm.at[:, 0], old, load_sem.at[2]),
        pltpu.make_async_copy(pore_hbm.at[0], pore, load_sem.at[3]),
        pltpu.make_async_copy(inv_hbm.at[:, :, 0], inv, load_sem.at[4]),
    ]
    for load in loads:
        load.start()

    barrier = pltpu.get_barrier_semaphore()

    @pl.loop(1, n)
    def _(step):
        pl.semaphore_signal(
            barrier, inc=1, device_id={"gx": lax.rem(me + step, n)}, device_id_type=MESH
        )

    cells = cells_ref[...]
    cell_y = cells // nz
    cell_z = cells - cell_y * nz
    at_y = [
        (lax.broadcasted_iota(jnp.int32, (ny, n), 0) == cell_y[k : k + 1]).astype(jnp.float32)
        for k in range(caps)
    ]
    at_z = [
        (lax.broadcasted_iota(jnp.int32, (nz, n), 0) == cell_z[k : k + 1]).astype(jnp.float32)
        for k in range(caps)
    ]

    def pick(plane, k):
        return jnp.sum(contract(plane, at_z[k], 1, 0) * at_y[k], axis=0, keepdims=True)

    wells = wells_ref[...]
    weights = jnp.where(wells >= 0, index_ref[...], 0.0)
    message[...] = jnp.zeros_like(message)
    message[caps : 2 * caps, :n] = weights
    message[2 * caps : 3 * caps, :n] = wells.astype(jnp.float32)
    message[3 * caps : 3 * caps + 1, :nwell] = rates_ref[...]
    loads[0].wait()
    for k in range(caps):
        message[k : k + 1, :n] = pick(u[0], k)
    inbox[me] = message[...]
    loads[1].wait()

    pl.semaphore_wait(barrier, n - 1)

    def well_copy(source_ref, box, sends, receives, step):
        target = lax.rem(me + step, n)
        return pltpu.make_async_remote_copy(
            src_ref=source_ref,
            dst_ref=box.at[me],
            send_sem=sends.at[target],
            recv_sem=receives.at[me],
            device_id={"gx": target},
            device_id_type=MESH,
        )

    def well_arrival(source_ref, box, sends, receives, step):
        origin = lax.rem(me + step, n)
        return pltpu.make_async_remote_copy(
            src_ref=source_ref,
            dst_ref=box.at[origin],
            send_sem=sends.at[origin],
            recv_sem=receives.at[origin],
            device_id={"gx": origin},
            device_id_type=MESH,
        )

    @pl.loop(1, n)
    def _(step):
        well_copy(message, inbox, well_send, well_recv, step).start()

    near = (me > 0, me < n - 1)
    place = (me - 1, me + 1)

    def bulk_copies(side, c):
        span = pl.ds(c * rows, rows)
        lands = 1 - side
        pairs = (
            (u.at[:, span], halo_u.at[lands, :, span]),
            (perm.at[span], halo_k.at[lands, span]),
        )
        return [
            pltpu.make_async_remote_copy(
                src_ref=src,
                dst_ref=dst,
                send_sem=bulk_send.at[side, c, i],
                recv_sem=bulk_recv.at[lands, c, i],
                device_id={"gx": place[side]},
                device_id_type=MESH,
            )
            for i, (src, dst) in enumerate(pairs)
        ]

    def tangent_copy(side, c):
        span = pl.ds(c * rows, rows)
        lands = 1 - side
        return pltpu.make_async_remote_copy(
            src_ref=send_d.at[:, span],
            dst_ref=halo_d.at[lands, :, span],
            send_sem=bulkd_send.at[side, c],
            recv_sem=bulkd_recv.at[lands, c],
            device_id={"gx": place[side]},
            device_id_type=MESH,
        )

    for c in range(CHUNKS):
        for side in range(2):

            @pl.when(near[side])
            def _(side=side, c=c):
                for copy in bulk_copies(side, c):
                    copy.start()

    for side in range(2):

        @pl.when(jnp.logical_not(near[side]))
        def _(side=side):
            halo_u[side] = jnp.zeros_like(halo_u[side])
            halo_k[side] = jnp.zeros_like(halo_k[side])
            halo_d[side] = jnp.zeros_like(halo_d[side])

    for load in loads[2:4]:
        load.wait()
    p, k_here = u[0], perm[...]
    f1, f2 = fractions(u[1], u[2])
    frac[0] = f1
    frac[1] = f2
    for i in range(3):
        tan = jnp.tanh(u[i])
        rise = 1.0 - tan * tan
        part[i] = pore[...] * (u[i] + 0.5 * tan - (old[i] + 0.5 * jnp.tanh(old[i])))
        accum[i] = pore[...] * (1.0 + 0.5 * rise)
        if i:
            slope[i - 1] = rise

    for axis, size in ((0, ny), (1, nz)):
        last = lax.broadcasted_iota(jnp.int32, (ny, nz), axis) == size - 1
        trans = transmissibility(k_here, pltpu.roll(k_here, size - 1, axis))
        trans = jnp.where(last, 0.0, trans)
        total = trans * (p - pltpu.roll(p, size - 1, axis))
        s1 = 0.5 * (f1 + pltpu.roll(f1, size - 1, axis))
        s2 = 0.5 * (f2 + pltpu.roll(f2, size - 1, axis))
        face[axis, 0] = trans
        face[axis, 1] = 0.5 * total
        face[axis, 2] = s1
        face[axis, 3] = s2
        flow1, flow2 = total * s1, total * s2
        flow0 = total - flow1 - flow2
        for i, flow in enumerate((flow0, flow1, flow2)):
            part[i] += flow - pltpu.roll(flow, 1, axis)

    @pl.loop(1, n)
    def _(step):
        well_arrival(message, inbox, well_send, well_recv, step).wait_recv()

    lane = lax.broadcasted_iota(jnp.int32, (n, n), 1)
    eye = (lax.broadcasted_iota(jnp.int32, (n, n), 0) == lane).astype(jnp.float32)
    mine = lane == me

    def turned(values):
        return contract(eye, values, 1, 1)

    def own(values):
        return jnp.sum(jnp.where(mine, values, 0.0), axis=1, keepdims=True)

    press = [turned(inbox[:, k, :n]) for k in range(caps)]
    weight = [inbox[:, caps + k, :n] for k in range(caps)]
    well = [inbox[:, 2 * caps + k, :n] for k in range(caps)]
    rates = inbox[:, 3 * caps, :nwell]
    well_lane = lax.broadcasted_iota(jnp.int32, (n, nwell), 1).astype(jnp.float32)
    my_weight, shares, flows = [], [], []
    for k in range(caps):
        my_well = own(well[k])
        live = my_well >= 0.0
        taken = [jnp.where(well[j] == my_well, weight[j], 0.0) for j in range(caps)]
        whole = sum(jnp.sum(t, axis=1, keepdims=True) for t in taken)
        inverse = 1.0 / jnp.where(live, whole, 1.0)
        rate = jnp.sum(jnp.where(well_lane == my_well, rates, 0.0), axis=1, keepdims=True)
        lift = sum(jnp.sum(t * b, axis=1, keepdims=True) for t, b in zip(taken, press))
        pull = jnp.where(live, own(weight[k]), 0.0)
        flows.append(pull * ((rate + lift) * inverse - own(press[k])))
        my_weight.append(pull)
        shares.append([t * inverse for t in taken])

    def spread(columns):
        plane = None
        for k in range(caps):
            line = jnp.sum(columns[k] * eye, axis=0, keepdims=True)
            term = contract(at_y[k] * line, at_z[k], 1, 1)
            plane = term if plane is None else plane + term
        return plane

    source[0] = spread(flows)

    row_mine = lax.broadcasted_iota(jnp.int32, (n, n), 0) == me
    own_well = lax.broadcasted_iota(jnp.int32, (nwell, n), 0)
    w_sum = jnp.zeros((nwell, 1), jnp.float32)
    p_sum = jnp.zeros((nwell, 1), jnp.float32)
    for k in range(caps):
        line = jnp.sum(jnp.where(row_mine, press[k], 0.0), axis=0, keepdims=True)
        hit = jnp.where(own_well == wells[k : k + 1], weights[k : k + 1], 0.0)
        w_sum += jnp.sum(hit, axis=1, keepdims=True)
        p_sum += jnp.sum(hit * line, axis=1, keepdims=True)
    square = lax.broadcasted_iota(jnp.int32, (nwell, nwell), 0) == lax.broadcasted_iota(
        jnp.int32, (nwell, nwell), 1
    )

    def as_row(column):
        return jnp.sum(jnp.where(square, column, 0.0), axis=0, keepdims=True)

    bottom_ref[...] = (rates_ref[...] + as_row(p_sum)) / as_row(w_sum)

    loads[4].wait()

    def blocks(span, r0, r1, r2):
        return [
            inv[i, 0, span] * r0 + inv[i, 1, span] * r1 + inv[i, 2, span] * r2 for i in range(3)
        ]

    for c in range(CHUNKS):
        span = pl.ds(c * rows, rows)
        for side in range(2):

            @pl.when(near[side])
            def _(side=side, c=c):
                for copy in bulk_copies(1 - side, c):
                    copy.wait_recv()

        p, f1, f2 = u[0, span], frac[0, span], frac[1, span]
        q = source[0, span]
        q1, q2 = q * f1, q * f2
        r0 = part[0, span] - (q - q1 - q2)
        r1 = part[1, span] - q1
        r2 = part[2, span] - q2
        for side in range(2):
            h1, h2 = fractions(halo_u[side, 1, span], halo_u[side, 2, span])
            trans = transmissibility(perm[span], halo_k[side, span])
            total = trans * (p - halo_u[side, 0, span])
            s1, s2 = 0.5 * (f1 + h1), 0.5 * (f2 + h2)
            edge[side, 0, span] = trans
            edge[side, 1, span] = 0.5 * total
            edge[side, 2, span] = s1
            edge[side, 3, span] = s2
            flow1, flow2 = total * s1, total * s2
            r0 += total - flow1 - flow2
            r1 += flow1
            r2 += flow2
        res_ref[0, 0, span] = r0
        res_ref[1, 0, span] = r1
        res_ref[2, 0, span] = r2
        d0, d1, d2 = blocks(span, -r0, -r1, -r2)
        g1, g2 = slope[0, span] * d1, slope[1, span] * d2
        mean = f1 * g1 + f2 * g2
        send_d[0, span] = d0
        send_d[1, span] = f1 * (g1 - mean)
        send_d[2, span] = f2 * (g2 - mean)
        corr[0, span] = d1
        corr[1, span] = d2
        for side in range(2):

            @pl.when(near[side])
            def _(side=side, c=c):
                tangent_copy(side, c).start()

    message_d[...] = jnp.zeros_like(message_d)
    for k in range(caps):
        message_d[k : k + 1, :n] = pick(send_d[0], k)
    inbox_d[me] = message_d[...]

    @pl.loop(1, n)
    def _(step):
        well_copy(message_d, inbox_d, welld_send, welld_recv, step).start()

    dp, df1, df2 = send_d[0], send_d[1], send_d[2]
    q = source[0]
    w1, w2 = q * df1, q * df2
    part[0] = res_ref[0, 0] + accum[0] * dp + (w1 + w2)
    part[1] = res_ref[1, 0] + accum[1] * corr[0] - w1
    part[2] = res_ref[2, 0] + accum[2] * corr[1] - w2
    for axis, size in ((0, ny), (1, nz)):
        total = face[axis, 0] * (dp - pltpu.roll(dp, size - 1, axis))
        flow1 = total * face[axis, 2] + face[axis, 1] * (df1 + pltpu.roll(df1, size - 1, axis))
        flow2 = total * face[axis, 3] + face[axis, 1] * (df2 + pltpu.roll(df2, size - 1, axis))
        flow0 = total - flow1 - flow2
        for i, flow in enumerate((flow0, flow1, flow2)):
            part[i] += flow - pltpu.roll(flow, 1, axis)

    @pl.loop(1, n)
    def _(step):
        well_arrival(message_d, inbox_d, welld_send, welld_recv, step).wait_recv()

    press = [turned(inbox_d[:, k, :n]) for k in range(caps)]
    flows = []
    for k in range(caps):
        lift = sum(jnp.sum(t * b, axis=1, keepdims=True) for t, b in zip(shares[k], press))
        flows.append(my_weight[k] * (lift - own(press[k])))
    source[1] = spread(flows)

    for c in range(CHUNKS):
        span = pl.ds(c * rows, rows)
        for side in range(2):

            @pl.when(near[side])
            def _(side=side, c=c):
                tangent_copy(1 - side, c).wait_recv()

        dp, df1, df2 = send_d[0, span], send_d[1, span], send_d[2, span]
        f1, f2 = frac[0, span], frac[1, span]
        q = source[1, span]
        q1, q2 = q * f1, q * f2
        r0 = part[0, span] - (q - q1 - q2)
        r1 = part[1, span] - q1
        r2 = part[2, span] - q2
        for side in range(2):
            total = edge[side, 0, span] * (dp - halo_d[side, 0, span])
            half = edge[side, 1, span]
            flow1 = total * edge[side, 2, span] + half * (df1 + halo_d[side, 1, span])
            flow2 = total * edge[side, 3, span] + half * (df2 + halo_d[side, 2, span])
            r0 += total - flow1 - flow2
            r1 += flow1
            r2 += flow2
        e0, e1, e2 = blocks(span, -r0, -r1, -r2)
        new_ref[0, 0, span] = u[0, span] + (dp + e0)
        new_ref[1, 0, span] = u[1, span] + (corr[0, span] + e1)
        new_ref[2, 0, span] = u[2, span] + (corr[1, span] + e2)

    for c in range(CHUNKS):
        for side in range(2):

            @pl.when(near[side])
            def _(side=side, c=c):
                for copy in bulk_copies(side, c):
                    copy.wait_send()
                tangent_copy(side, c).wait_send()

    @pl.loop(1, n)
    def _(step):
        well_copy(message, inbox, well_send, well_recv, step).wait_send()
        well_copy(message_d, inbox_d, welld_send, welld_recv, step).wait_send()


def shards(
    state,
    old_state,
    pore_volume,
    permeability,
    inverse_blocks,
    perf_cells,
    perf_wells,
    well_index,
    well_rates,
):
    n = lax.axis_size("gx")
    ny, nz = state.shape[2:]
    caps = perf_cells.shape[0]
    lines = -(-(3 * caps + 1) // 8) * 8
    width = -(-max(n, well_rates.shape[0]) // 128) * 128
    any_spec = pl.BlockSpec(memory_space=pl.ANY)
    vmem_spec = pl.BlockSpec(memory_space=pltpu.VMEM)

    def planes(*lead):
        return pltpu.VMEM((*lead, ny, nz), jnp.float32)

    dma = pltpu.SemaphoreType.DMA
    new_state, residual, bottom = pl.pallas_call(
        functools.partial(kernel, n),
        out_shape=(
            jax.ShapeDtypeStruct(state.shape, jnp.float32),
            jax.ShapeDtypeStruct(state.shape, jnp.float32),
            jax.ShapeDtypeStruct((1, well_rates.shape[0]), jnp.float32),
        ),
        in_specs=[any_spec] * 5 + [vmem_spec] * 4,
        out_specs=(vmem_spec, vmem_spec, vmem_spec),
        scratch_shapes=[
            planes(3),
            planes(3),
            planes(),
            planes(),
            planes(3, 3),
            planes(2, 3),
            planes(2),
            planes(2, 3),
            planes(3),
            planes(2),
            planes(2),
            planes(2),
            planes(3),
            planes(2, 4),
            planes(2, 4),
            planes(3),
            planes(2),
            pltpu.VMEM((lines, width), jnp.float32),
            pltpu.VMEM((n, lines, width), jnp.float32),
            pltpu.VMEM((caps, width), jnp.float32),
            pltpu.VMEM((n, caps, width), jnp.float32),
            dma((5,)),
            dma((n,)),
            dma((n,)),
            dma((n,)),
            dma((n,)),
            dma((2, CHUNKS, 2)),
            dma((2, CHUNKS, 2)),
            dma((2, CHUNKS)),
            dma((2, CHUNKS)),
        ],
        compiler_params=pltpu.CompilerParams(
            collective_id=0, has_side_effects=True, vmem_limit_bytes=40 * 1024 * 1024
        ),
    )(
        state,
        old_state,
        pore_volume,
        permeability,
        inverse_blocks,
        perf_cells,
        perf_wells,
        well_index,
        well_rates.reshape(1, -1),
    )
    return new_state, residual, bottom.reshape(-1)


def solution(mesh):
    return jax.shard_map(
        shards,
        mesh=mesh,
        in_specs=(
            P(None, ("groups", "gx"), None, None),
            P(None, ("groups", "gx"), None, None),
            P(("groups", "gx"), None, None),
            P(("groups", "gx"), None, None),
            P(None, None, ("groups", "gx"), None, None),
            P(None, ("groups", "gx")),
            P(None, ("groups", "gx")),
            P(None, ("groups", "gx")),
            P(("groups", "gx")),
        ),
        out_specs=(
            P(None, ("groups", "gx"), None, None),
            P(None, ("groups", "gx"), None, None),
            P(("groups", "gx")),
        ),
        check_vma=False,
    )
```

```python
import functools

import jax
import jax.numpy as jnp
from jax import lax
from jax.experimental import pallas as pl
from jax.experimental.pallas import tpu as pltpu
from jax.sharding import PartitionSpec as P

CHUNKS = 4
VMEM_LIMIT = 62 * 1024 * 1024
MESH = pl.DeviceIdType.MESH
EXACT = lax.Precision.HIGHEST


def contract(left, right, left_dim, right_dim):
    return lax.dot_general(
        left,
        right,
        (((left_dim,), (right_dim,)), ((), ())),
        precision=EXACT,
        preferred_element_type=jnp.float32,
    )


def fractions(first, second):
    e1 = jnp.exp(jnp.tanh(first))
    e2 = jnp.exp(jnp.tanh(second))
    inverse = 1.0 / (1.0 + e1 + e2)
    return e1 * inverse, e2 * inverse


def transmissibility(k_a, k_b):
    return 2.0 * k_a * k_b / (k_a + k_b)


def kernel(
    n,
    state_hbm,
    old_hbm,
    pore_hbm,
    perm_hbm,
    inv_hbm,
    cells_hbm,
    wells_hbm,
    index_hbm,
    rates_hbm,
    new_hbm,
    res_hbm,
    bottom_hbm,
    new_ref,
    res_ref,
    bottom_ref,
    save_sem,
    u,
    old,
    pore,
    perm,
    inv,
    cells_ref,
    wells_ref,
    index_ref,
    rates_ref,
    halo_u,
    halo_k,
    halo_d,
    send_d,
    corr,
    frac,
    slope,
    accum,
    face,
    edge,
    part,
    source,
    message,
    inbox,
    message_d,
    inbox_d,
    load_sem,
    well_send,
    well_recv,
    welld_send,
    welld_recv,
    bulk_send,
    bulk_recv,
    bulkd_send,
    bulkd_recv,
):
    me = lax.axis_index("gx")
    ny, nz = perm.shape
    rows = ny // CHUNKS
    caps = cells_ref.shape[0]
    nwell = rates_ref.shape[1]

    loads = [
        pltpu.make_async_copy(state_hbm.at[:, 0], u, load_sem.at[0]),
        pltpu.make_async_copy(perm_hbm.at[0], perm, load_sem.at[1]),
        pltpu.make_async_copy(old_hbm.at[:, 0], old, load_sem.at[2]),
        pltpu.make_async_copy(pore_hbm.at[0], pore, load_sem.at[3]),
        pltpu.make_async_copy(inv_hbm.at[:, :, 0], inv, load_sem.at[4]),
        pltpu.make_async_copy(cells_hbm, cells_ref, load_sem.at[5]),
        pltpu.make_async_copy(wells_hbm, wells_ref, load_sem.at[6]),
        pltpu.make_async_copy(index_hbm, index_ref, load_sem.at[7]),
        pltpu.make_async_copy(rates_hbm, rates_ref, load_sem.at[8]),
    ]
    for load in loads[5:] + loads[:5]:
        load.start()

    saves = [pltpu.make_async_copy(bottom_ref, bottom_hbm, save_sem.at[2 * CHUNKS])]

    def save(source_ref, target_ref, span, slot):
        copy = pltpu.make_async_copy(
            source_ref.at[:, :, span], target_ref.at[:, :, span], save_sem.at[slot]
        )
        copy.start()
        saves.append(copy)

    barrier = pltpu.get_barrier_semaphore()

    @pl.loop(1, n)
    def _(step):
        pl.semaphore_signal(
            barrier, inc=1, device_id={"gx": lax.rem(me + step, n)}, device_id_type=MESH
        )

    for load in loads[5:]:
        load.wait()
    cells = cells_ref[...]
    cell_y = cells // nz
    cell_z = cells - cell_y * nz
    at_y = [
        (lax.broadcasted_iota(jnp.int32, (ny, n), 0) == cell_y[k : k + 1]).astype(jnp.float32)
        for k in range(caps)
    ]
    at_z = [
        (lax.broadcasted_iota(jnp.int32, (nz, n), 0) == cell_z[k : k + 1]).astype(jnp.float32)
        for k in range(caps)
    ]

    def pick(plane, k):
        return jnp.sum(contract(plane, at_z[k], 1, 0) * at_y[k], axis=0, keepdims=True)

    wells = wells_ref[...]
    weights = jnp.where(wells >= 0, index_ref[...], 0.0)
    message[...] = jnp.zeros_like(message)
    message[caps : 2 * caps, :n] = weights
    message[2 * caps : 3 * caps, :n] = wells.astype(jnp.float32)
    message[3 * caps : 3 * caps + 1, :nwell] = rates_ref[...]
    loads[0].wait()
    for k in range(caps):
        message[k : k + 1, :n] = pick(u[0], k)
    inbox[me] = message[...]
    loads[1].wait()

    pl.semaphore_wait(barrier, n - 1)

    def well_copy(source_ref, box, sends, receives, step):
        target = lax.rem(me + step, n)
        return pltpu.make_async_remote_copy(
            src_ref=source_ref,
            dst_ref=box.at[me],
            send_sem=sends.at[target],
            recv_sem=receives.at[me],
            device_id={"gx": target},
            device_id_type=MESH,
        )

    def well_arrival(source_ref, box, sends, receives, step):
        origin = lax.rem(me + step, n)
        return pltpu.make_async_remote_copy(
            src_ref=source_ref,
            dst_ref=box.at[origin],
            send_sem=sends.at[origin],
            recv_sem=receives.at[origin],
            device_id={"gx": origin},
            device_id_type=MESH,
        )

    @pl.loop(1, n)
    def _(step):
        well_copy(message, inbox, well_send, well_recv, step).start()

    near = (me > 0, me < n - 1)
    place = (me - 1, me + 1)

    def bulk_copies(side, c):
        span = pl.ds(c * rows, rows)
        lands = 1 - side
        pairs = (
            (u.at[:, span], halo_u.at[lands, :, span]),
            (perm.at[span], halo_k.at[lands, span]),
        )
        return [
            pltpu.make_async_remote_copy(
                src_ref=src,
                dst_ref=dst,
                send_sem=bulk_send.at[side, c, i],
                recv_sem=bulk_recv.at[lands, c, i],
                device_id={"gx": place[side]},
                device_id_type=MESH,
            )
            for i, (src, dst) in enumerate(pairs)
        ]

    def tangent_copy(side, c):
        span = pl.ds(c * rows, rows)
        lands = 1 - side
        return pltpu.make_async_remote_copy(
            src_ref=send_d.at[:, span],
            dst_ref=halo_d.at[lands, :, span],
            send_sem=bulkd_send.at[side, c],
            recv_sem=bulkd_recv.at[lands, c],
            device_id={"gx": place[side]},
            device_id_type=MESH,
        )

    for c in range(CHUNKS):
        for side in range(2):

            @pl.when(near[side])
            def _(side=side, c=c):
                for copy in bulk_copies(side, c):
                    copy.start()

    for side in range(2):

        @pl.when(jnp.logical_not(near[side]))
        def _(side=side):
            halo_u[side] = jnp.zeros_like(halo_u[side])
            halo_k[side] = jnp.zeros_like(halo_k[side])
            halo_d[side] = jnp.zeros_like(halo_d[side])

    for load in loads[2:4]:
        load.wait()
    p, k_here = u[0], perm[...]
    f1, f2 = fractions(u[1], u[2])
    frac[0] = f1
    frac[1] = f2
    for i in range(3):
        tan = jnp.tanh(u[i])
        rise = 1.0 - tan * tan
        part[i] = pore[...] * (u[i] + 0.5 * tan - (old[i] + 0.5 * jnp.tanh(old[i])))
        accum[i] = pore[...] * (1.0 + 0.5 * rise)
        if i:
            slope[i - 1] = rise

    for axis, size in ((0, ny), (1, nz)):
        last = lax.broadcasted_iota(jnp.int32, (ny, nz), axis) == size - 1
        trans = transmissibility(k_here, pltpu.roll(k_here, size - 1, axis))
        trans = jnp.where(last, 0.0, trans)
        total = trans * (p - pltpu.roll(p, size - 1, axis))
        s1 = 0.5 * (f1 + pltpu.roll(f1, size - 1, axis))
        s2 = 0.5 * (f2 + pltpu.roll(f2, size - 1, axis))
        face[axis, 0] = trans
        face[axis, 1] = 0.5 * total
        face[axis, 2] = s1
        face[axis, 3] = s2
        flow1, flow2 = total * s1, total * s2
        flow0 = total - flow1 - flow2
        for i, flow in enumerate((flow0, flow1, flow2)):
            part[i] += flow - pltpu.roll(flow, 1, axis)

    @pl.loop(1, n)
    def _(step):
        well_arrival(message, inbox, well_send, well_recv, step).wait_recv()

    lane = lax.broadcasted_iota(jnp.int32, (n, n), 1)
    eye = (lax.broadcasted_iota(jnp.int32, (n, n), 0) == lane).astype(jnp.float32)
    mine = lane == me

    def turned(values):
        return contract(eye, values, 1, 1)

    def own(values):
        return jnp.sum(jnp.where(mine, values, 0.0), axis=1, keepdims=True)

    press = [turned(inbox[:, k, :n]) for k in range(caps)]
    weight = [inbox[:, caps + k, :n] for k in range(caps)]
    well = [inbox[:, 2 * caps + k, :n] for k in range(caps)]
    rates = inbox[:, 3 * caps, :nwell]
    well_lane = lax.broadcasted_iota(jnp.int32, (n, nwell), 1).astype(jnp.float32)
    my_weight, shares, flows = [], [], []
    for k in range(caps):
        my_well = own(well[k])
        live = my_well >= 0.0
        taken = [jnp.where(well[j] == my_well, weight[j], 0.0) for j in range(caps)]
        whole = sum(jnp.sum(t, axis=1, keepdims=True) for t in taken)
        inverse = 1.0 / jnp.where(live, whole, 1.0)
        rate = jnp.sum(jnp.where(well_lane == my_well, rates, 0.0), axis=1, keepdims=True)
        lift = sum(jnp.sum(t * b, axis=1, keepdims=True) for t, b in zip(taken, press))
        pull = jnp.where(live, own(weight[k]), 0.0)
        flows.append(pull * ((rate + lift) * inverse - own(press[k])))
        my_weight.append(pull)
        shares.append([t * inverse for t in taken])

    def spread(columns):
        plane = None
        for k in range(caps):
            line = jnp.sum(columns[k] * eye, axis=0, keepdims=True)
            term = contract(at_y[k] * line, at_z[k], 1, 1)
            plane = term if plane is None else plane + term
        return plane

    source[0] = spread(flows)

    row_mine = lax.broadcasted_iota(jnp.int32, (n, n), 0) == me
    own_well = lax.broadcasted_iota(jnp.int32, (nwell, n), 0)
    w_sum = jnp.zeros((nwell, 1), jnp.float32)
    p_sum = jnp.zeros((nwell, 1), jnp.float32)
    for k in range(caps):
        line = jnp.sum(jnp.where(row_mine, press[k], 0.0), axis=0, keepdims=True)
        hit = jnp.where(own_well == wells[k : k + 1], weights[k : k + 1], 0.0)
        w_sum += jnp.sum(hit, axis=1, keepdims=True)
        p_sum += jnp.sum(hit * line, axis=1, keepdims=True)
    square = lax.broadcasted_iota(jnp.int32, (nwell, nwell), 0) == lax.broadcasted_iota(
        jnp.int32, (nwell, nwell), 1
    )

    def as_row(column):
        return jnp.sum(jnp.where(square, column, 0.0), axis=0, keepdims=True)

    bottom_ref[...] = (rates_ref[...] + as_row(p_sum)) / as_row(w_sum)
    saves[0].start()

    loads[4].wait()

    def blocks(span, r0, r1, r2):
        return [
            inv[i, 0, span] * r0 + inv[i, 1, span] * r1 + inv[i, 2, span] * r2 for i in range(3)
        ]

    for c in range(CHUNKS):
        span = pl.ds(c * rows, rows)
        for side in range(2):

            @pl.when(near[side])
            def _(side=side, c=c):
                for copy in bulk_copies(1 - side, c):
                    copy.wait_recv()

        p, f1, f2 = u[0, span], frac[0, span], frac[1, span]
        q = source[0, span]
        q1, q2 = q * f1, q * f2
        r0 = part[0, span] - (q - q1 - q2)
        r1 = part[1, span] - q1
        r2 = part[2, span] - q2
        for side in range(2):
            h1, h2 = fractions(halo_u[side, 1, span], halo_u[side, 2, span])
            trans = transmissibility(perm[span], halo_k[side, span])
            total = trans * (p - halo_u[side, 0, span])
            s1, s2 = 0.5 * (f1 + h1), 0.5 * (f2 + h2)
            edge[side, 0, span] = trans
            edge[side, 1, span] = 0.5 * total
            edge[side, 2, span] = s1
            edge[side, 3, span] = s2
            flow1, flow2 = total * s1, total * s2
            r0 += total - flow1 - flow2
            r1 += flow1
            r2 += flow2
        res_ref[0, 0, span] = r0
        res_ref[1, 0, span] = r1
        res_ref[2, 0, span] = r2
        save(res_ref, res_hbm, span, c)
        d0, d1, d2 = blocks(span, -r0, -r1, -r2)
        g1, g2 = slope[0, span] * d1, slope[1, span] * d2
        mean = f1 * g1 + f2 * g2
        send_d[0, span] = d0
        send_d[1, span] = f1 * (g1 - mean)
        send_d[2, span] = f2 * (g2 - mean)
        corr[0, span] = d1
        corr[1, span] = d2
        for side in range(2):

            @pl.when(near[side])
            def _(side=side, c=c):
                tangent_copy(side, c).start()

    message_d[...] = jnp.zeros_like(message_d)
    for k in range(caps):
        message_d[k : k + 1, :n] = pick(send_d[0], k)
    inbox_d[me] = message_d[...]

    @pl.loop(1, n)
    def _(step):
        well_copy(message_d, inbox_d, welld_send, welld_recv, step).start()

    dp, df1, df2 = send_d[0], send_d[1], send_d[2]
    q = source[0]
    w1, w2 = q * df1, q * df2
    part[0] = res_ref[0, 0] + accum[0] * dp + (w1 + w2)
    part[1] = res_ref[1, 0] + accum[1] * corr[0] - w1
    part[2] = res_ref[2, 0] + accum[2] * corr[1] - w2
    for axis, size in ((0, ny), (1, nz)):
        total = face[axis, 0] * (dp - pltpu.roll(dp, size - 1, axis))
        flow1 = total * face[axis, 2] + face[axis, 1] * (df1 + pltpu.roll(df1, size - 1, axis))
        flow2 = total * face[axis, 3] + face[axis, 1] * (df2 + pltpu.roll(df2, size - 1, axis))
        flow0 = total - flow1 - flow2
        for i, flow in enumerate((flow0, flow1, flow2)):
            part[i] += flow - pltpu.roll(flow, 1, axis)

    @pl.loop(1, n)
    def _(step):
        well_arrival(message_d, inbox_d, welld_send, welld_recv, step).wait_recv()

    press = [turned(inbox_d[:, k, :n]) for k in range(caps)]
    flows = []
    for k in range(caps):
        lift = sum(jnp.sum(t * b, axis=1, keepdims=True) for t, b in zip(shares[k], press))
        flows.append(my_weight[k] * (lift - own(press[k])))
    source[1] = spread(flows)

    for c in range(CHUNKS):
        span = pl.ds(c * rows, rows)
        for side in range(2):

            @pl.when(near[side])
            def _(side=side, c=c):
                tangent_copy(1 - side, c).wait_recv()

        dp, df1, df2 = send_d[0, span], send_d[1, span], send_d[2, span]
        f1, f2 = frac[0, span], frac[1, span]
        q = source[1, span]
        q1, q2 = q * f1, q * f2
        r0 = part[0, span] - (q - q1 - q2)
        r1 = part[1, span] - q1
        r2 = part[2, span] - q2
        for side in range(2):
            total = edge[side, 0, span] * (dp - halo_d[side, 0, span])
            half = edge[side, 1, span]
            flow1 = total * edge[side, 2, span] + half * (df1 + halo_d[side, 1, span])
            flow2 = total * edge[side, 3, span] + half * (df2 + halo_d[side, 2, span])
            r0 += total - flow1 - flow2
            r1 += flow1
            r2 += flow2
        e0, e1, e2 = blocks(span, -r0, -r1, -r2)
        new_ref[0, 0, span] = u[0, span] + (dp + e0)
        new_ref[1, 0, span] = u[1, span] + (corr[0, span] + e1)
        new_ref[2, 0, span] = u[2, span] + (corr[1, span] + e2)
        save(new_ref, new_hbm, span, CHUNKS + c)

    for copy in saves:
        copy.wait()

    for c in range(CHUNKS):
        for side in range(2):

            @pl.when(near[side])
            def _(side=side, c=c):
                for copy in bulk_copies(side, c):
                    copy.wait_send()
                tangent_copy(side, c).wait_send()

    @pl.loop(1, n)
    def _(step):
        well_copy(message, inbox, well_send, well_recv, step).wait_send()
        well_copy(message_d, inbox_d, welld_send, welld_recv, step).wait_send()


def store(*refs):
    copies = [
        pltpu.make_async_copy(refs[i], refs[3 + i], refs[6].at[i]) for i in range(3)
    ]
    for copy in copies:
        copy.start()
    for copy in copies:
        copy.wait()


def shards(
    state,
    old_state,
    pore_volume,
    permeability,
    inverse_blocks,
    perf_cells,
    perf_wells,
    well_index,
    well_rates,
):
    n = lax.axis_size("gx")
    ny, nz = state.shape[2:]
    caps = perf_cells.shape[0]
    lines = -(-(3 * caps + 1) // 8) * 8
    width = -(-max(n, well_rates.shape[0]) // 128) * 128
    hbm_spec = pl.BlockSpec(memory_space=pltpu.HBM)

    def planes(*lead):
        return pltpu.VMEM((*lead, ny, nz), jnp.float32)

    dma = pltpu.SemaphoreType.DMA
    out_shape = (
        jax.ShapeDtypeStruct(state.shape, jnp.float32),
        jax.ShapeDtypeStruct(state.shape, jnp.float32),
        jax.ShapeDtypeStruct((1, well_rates.shape[0]), jnp.float32),
    )
    results = pl.pallas_call(
        functools.partial(kernel, n),
        out_shape=out_shape,
        in_specs=[hbm_spec] * 9,
        out_specs=(hbm_spec,) * 3,
        scratch_shapes=[
            planes(3, 1),
            planes(3, 1),
            pltpu.VMEM((1, well_rates.shape[0]), jnp.float32),
            dma((2 * CHUNKS + 1,)),
            planes(3),
            planes(3),
            planes(),
            planes(),
            planes(3, 3),
            pltpu.VMEM(perf_cells.shape, jnp.int32),
            pltpu.VMEM(perf_wells.shape, jnp.int32),
            pltpu.VMEM(well_index.shape, jnp.float32),
            pltpu.VMEM((1, well_rates.shape[0]), jnp.float32),
            planes(2, 3),
            planes(2),
            planes(2, 3),
            planes(3),
            planes(2),
            planes(2),
            planes(2),
            planes(3),
            planes(2, 4),
            planes(2, 4),
            planes(3),
            planes(2),
            pltpu.VMEM((lines, width), jnp.float32),
            pltpu.VMEM((n, lines, width), jnp.float32),
            pltpu.VMEM((caps, width), jnp.float32),
            pltpu.VMEM((n, caps, width), jnp.float32),
            dma((9,)),
            dma((n,)),
            dma((n,)),
            dma((n,)),
            dma((n,)),
            dma((2, CHUNKS, 2)),
            dma((2, CHUNKS, 2)),
            dma((2, CHUNKS)),
            dma((2, CHUNKS)),
        ],
        compiler_params=pltpu.CompilerParams(
            collective_id=0, has_side_effects=True, vmem_limit_bytes=VMEM_LIMIT
        ),
    )(
        state,
        old_state,
        pore_volume,
        permeability,
        inverse_blocks,
        perf_cells,
        perf_wells,
        well_index,
        well_rates.reshape(1, -1),
    )
    new_state, residual, bottom = pl.pallas_call(
        store,
        out_shape=out_shape,
        in_specs=[pl.BlockSpec(memory_space=pl.ANY)] * 3,
        out_specs=(hbm_spec,) * 3,
        scratch_shapes=[dma((3,))],
        compiler_params=pltpu.CompilerParams(vmem_limit_bytes=VMEM_LIMIT),
    )(*results)
    return new_state, residual, bottom.reshape(-1)


def solution(mesh):
    return jax.shard_map(
        shards,
        mesh=mesh,
        in_specs=(
            P(None, ("groups", "gx"), None, None),
            P(None, ("groups", "gx"), None, None),
            P(("groups", "gx"), None, None),
            P(("groups", "gx"), None, None),
            P(None, None, ("groups", "gx"), None, None),
            P(None, ("groups", "gx")),
            P(None, ("groups", "gx")),
            P(None, ("groups", "gx")),
            P(("groups", "gx")),
        ),
        out_specs=(
            P(None, ("groups", "gx"), None, None),
            P(None, ("groups", "gx"), None, None),
            P(("groups", "gx")),
        ),
        check_vma=False,
    )
```

```python
import functools

import jax
import jax.numpy as jnp
from jax import lax
from jax.experimental import pallas as pl
from jax.experimental.pallas import tpu as pltpu
from jax.sharding import PartitionSpec as P

CHUNKS = 4
VMEM_LIMIT = 62 * 1024 * 1024
MESH = pl.DeviceIdType.MESH
EXACT = lax.Precision.HIGHEST


def contract(left, right, left_dim, right_dim):
    return lax.dot_general(
        left,
        right,
        (((left_dim,), (right_dim,)), ((), ())),
        precision=EXACT,
        preferred_element_type=jnp.float32,
    )


def fractions(first, second):
    e1 = jnp.exp(jnp.tanh(first))
    e2 = jnp.exp(jnp.tanh(second))
    inverse = 1.0 / (1.0 + e1 + e2)
    return e1 * inverse, e2 * inverse


def transmissibility(k_a, k_b):
    return 2.0 * k_a * k_b / (k_a + k_b)


def kernel(
    n,
    state_hbm,
    old_hbm,
    pore_hbm,
    perm_hbm,
    inv_hbm,
    cells_hbm,
    wells_hbm,
    index_hbm,
    rates_hbm,
    new_hbm,
    res_hbm,
    bottom_hbm,
    new_ref,
    res_ref,
    bottom_ref,
    save_sem,
    u,
    old,
    pore,
    perm,
    inv,
    cells_ref,
    wells_ref,
    index_ref,
    rates_ref,
    halo_u,
    halo_k,
    halo_d,
    send_d,
    corr,
    frac,
    slope,
    accum,
    face,
    edge,
    part,
    source,
    message,
    inbox,
    message_d,
    inbox_d,
    load_sem,
    well_send,
    well_recv,
    welld_send,
    welld_recv,
    bulk_send,
    bulk_recv,
    bulkd_send,
    bulkd_recv,
):
    me = lax.axis_index("gx")
    ny, nz = perm.shape
    rows = ny // CHUNKS
    caps = cells_ref.shape[0]
    nwell = rates_ref.shape[1]

    loads = [
        pltpu.make_async_copy(state_hbm.at[:, 0], u, load_sem.at[0]),
        pltpu.make_async_copy(perm_hbm.at[0], perm, load_sem.at[1]),
        pltpu.make_async_copy(old_hbm.at[:, 0], old, load_sem.at[2]),
        pltpu.make_async_copy(pore_hbm.at[0], pore, load_sem.at[3]),
        pltpu.make_async_copy(inv_hbm.at[:, :, 0], inv, load_sem.at[4]),
        pltpu.make_async_copy(cells_hbm, cells_ref, load_sem.at[5]),
        pltpu.make_async_copy(wells_hbm, wells_ref, load_sem.at[6]),
        pltpu.make_async_copy(index_hbm, index_ref, load_sem.at[7]),
        pltpu.make_async_copy(rates_hbm, rates_ref, load_sem.at[8]),
    ]
    for load in loads[5:] + loads[:5]:
        load.start()

    saves = [pltpu.make_async_copy(bottom_ref, bottom_hbm, save_sem.at[2 * CHUNKS])]

    def save(source_ref, target_ref, span, slot):
        copy = pltpu.make_async_copy(
            source_ref.at[:, :, span], target_ref.at[:, :, span], save_sem.at[slot]
        )
        copy.start()
        saves.append(copy)

    barrier = pltpu.get_barrier_semaphore()

    @pl.loop(1, n)
    def _(step):
        pl.semaphore_signal(
            barrier, inc=1, device_id={"gx": lax.rem(me + step, n)}, device_id_type=MESH
        )

    for load in loads[5:]:
        load.wait()
    cells = cells_ref[...]
    cell_y = cells // nz
    cell_z = cells - cell_y * nz
    at_y = [
        (lax.broadcasted_iota(jnp.int32, (ny, n), 0) == cell_y[k : k + 1]).astype(jnp.float32)
        for k in range(caps)
    ]
    at_z = [
        (lax.broadcasted_iota(jnp.int32, (nz, n), 0) == cell_z[k : k + 1]).astype(jnp.float32)
        for k in range(caps)
    ]

    def pick(plane, k):
        return jnp.sum(contract(plane, at_z[k], 1, 0) * at_y[k], axis=0, keepdims=True)

    wells = wells_ref[...]
    weights = jnp.where(wells >= 0, index_ref[...], 0.0)
    message[...] = jnp.zeros_like(message)
    message[caps : 2 * caps, :n] = weights
    message[2 * caps : 3 * caps, :n] = wells.astype(jnp.float32)
    message[3 * caps : 3 * caps + 1, :nwell] = rates_ref[...]
    loads[0].wait()
    for k in range(caps):
        message[k : k + 1, :n] = pick(u[0], k)
    inbox[me] = message[...]
    loads[1].wait()

    pl.semaphore_wait(barrier, n - 1)

    def well_copy(source_ref, box, sends, receives, step):
        target = lax.rem(me + step, n)
        return pltpu.make_async_remote_copy(
            src_ref=source_ref,
            dst_ref=box.at[me],
            send_sem=sends.at[target],
            recv_sem=receives.at[me],
            device_id={"gx": target},
            device_id_type=MESH,
        )

    def well_arrival(source_ref, box, sends, receives, step):
        origin = lax.rem(me + step, n)
        return pltpu.make_async_remote_copy(
            src_ref=source_ref,
            dst_ref=box.at[origin],
            send_sem=sends.at[origin],
            recv_sem=receives.at[origin],
            device_id={"gx": origin},
            device_id_type=MESH,
        )

    @pl.loop(1, n)
    def _(step):
        well_copy(message, inbox, well_send, well_recv, step).start()

    near = (me > 0, me < n - 1)
    place = (me - 1, me + 1)

    def bulk_copies(side, c):
        span = pl.ds(c * rows, rows)
        lands = 1 - side
        pairs = (
            (u.at[:, span], halo_u.at[lands, :, span]),
            (perm.at[span], halo_k.at[lands, span]),
        )
        return [
            pltpu.make_async_remote_copy(
                src_ref=src,
                dst_ref=dst,
                send_sem=bulk_send.at[side, c, i],
                recv_sem=bulk_recv.at[lands, c, i],
                device_id={"gx": place[side]},
                device_id_type=MESH,
            )
            for i, (src, dst) in enumerate(pairs)
        ]

    def tangent_copy(side, c):
        span = pl.ds(c * rows, rows)
        lands = 1 - side
        return pltpu.make_async_remote_copy(
            src_ref=send_d.at[:, span],
            dst_ref=halo_d.at[lands, :, span],
            send_sem=bulkd_send.at[side, c],
            recv_sem=bulkd_recv.at[lands, c],
            device_id={"gx": place[side]},
            device_id_type=MESH,
        )

    for c in range(CHUNKS):
        for side in range(2):

            @pl.when(near[side])
            def _(side=side, c=c):
                for copy in bulk_copies(side, c):
                    copy.start()

    for side in range(2):

        @pl.when(jnp.logical_not(near[side]))
        def _(side=side):
            halo_u[side] = jnp.zeros_like(halo_u[side])
            halo_k[side] = jnp.zeros_like(halo_k[side])
            halo_d[side] = jnp.zeros_like(halo_d[side])

    for load in loads[2:4]:
        load.wait()
    p, k_here = u[0], perm[...]
    f1, f2 = fractions(u[1], u[2])
    frac[0] = f1
    frac[1] = f2
    for i in range(3):
        tan = jnp.tanh(u[i])
        rise = 1.0 - tan * tan
        part[i] = pore[...] * (u[i] + 0.5 * tan - (old[i] + 0.5 * jnp.tanh(old[i])))
        accum[i] = pore[...] * (1.0 + 0.5 * rise)
        if i:
            slope[i - 1] = rise

    for axis, size in ((0, ny), (1, nz)):
        last = lax.broadcasted_iota(jnp.int32, (ny, nz), axis) == size - 1
        trans = transmissibility(k_here, pltpu.roll(k_here, size - 1, axis))
        trans = jnp.where(last, 0.0, trans)
        total = trans * (p - pltpu.roll(p, size - 1, axis))
        s1 = 0.5 * (f1 + pltpu.roll(f1, size - 1, axis))
        s2 = 0.5 * (f2 + pltpu.roll(f2, size - 1, axis))
        face[axis, 0] = trans
        face[axis, 1] = 0.5 * total
        face[axis, 2] = s1
        face[axis, 3] = s2
        flow1, flow2 = total * s1, total * s2
        flow0 = total - flow1 - flow2
        for i, flow in enumerate((flow0, flow1, flow2)):
            part[i] += flow - pltpu.roll(flow, 1, axis)

    @pl.loop(1, n)
    def _(step):
        well_arrival(message, inbox, well_send, well_recv, step).wait_recv()

    lane = lax.broadcasted_iota(jnp.int32, (n, n), 1)
    eye = (lax.broadcasted_iota(jnp.int32, (n, n), 0) == lane).astype(jnp.float32)
    mine = lane == me

    def turned(values):
        return contract(eye, values, 1, 1)

    def own(values):
        return jnp.sum(jnp.where(mine, values, 0.0), axis=1, keepdims=True)

    press = [turned(inbox[:, k, :n]) for k in range(caps)]
    weight = [inbox[:, caps + k, :n] for k in range(caps)]
    well = [inbox[:, 2 * caps + k, :n] for k in range(caps)]
    rates = inbox[:, 3 * caps, :nwell]
    well_lane = lax.broadcasted_iota(jnp.int32, (n, nwell), 1).astype(jnp.float32)
    my_weight, shares, flows = [], [], []
    for k in range(caps):
        my_well = own(well[k])
        live = my_well >= 0.0
        taken = [jnp.where(well[j] == my_well, weight[j], 0.0) for j in range(caps)]
        whole = sum(jnp.sum(t, axis=1, keepdims=True) for t in taken)
        inverse = 1.0 / jnp.where(live, whole, 1.0)
        rate = jnp.sum(jnp.where(well_lane == my_well, rates, 0.0), axis=1, keepdims=True)
        lift = sum(jnp.sum(t * b, axis=1, keepdims=True) for t, b in zip(taken, press))
        pull = jnp.where(live, own(weight[k]), 0.0)
        flows.append(pull * ((rate + lift) * inverse - own(press[k])))
        my_weight.append(pull)
        shares.append([t * inverse for t in taken])

    def spread(columns):
        plane = None
        for k in range(caps):
            line = jnp.sum(columns[k] * eye, axis=0, keepdims=True)
            term = contract(at_y[k] * line, at_z[k], 1, 1)
            plane = term if plane is None else plane + term
        return plane

    source[0] = spread(flows)

    row_mine = lax.broadcasted_iota(jnp.int32, (n, n), 0) == me
    own_well = lax.broadcasted_iota(jnp.int32, (nwell, n), 0)
    w_sum = jnp.zeros((nwell, 1), jnp.float32)
    p_sum = jnp.zeros((nwell, 1), jnp.float32)
    for k in range(caps):
        line = jnp.sum(jnp.where(row_mine, press[k], 0.0), axis=0, keepdims=True)
        hit = jnp.where(own_well == wells[k : k + 1], weights[k : k + 1], 0.0)
        w_sum += jnp.sum(hit, axis=1, keepdims=True)
        p_sum += jnp.sum(hit * line, axis=1, keepdims=True)
    square = lax.broadcasted_iota(jnp.int32, (nwell, nwell), 0) == lax.broadcasted_iota(
        jnp.int32, (nwell, nwell), 1
    )

    def as_row(column):
        return jnp.sum(jnp.where(square, column, 0.0), axis=0, keepdims=True)

    bottom_ref[...] = (rates_ref[...] + as_row(p_sum)) / as_row(w_sum)
    saves[0].start()

    loads[4].wait()

    def blocks(span, r0, r1, r2):
        return [
            inv[i, 0, span] * r0 + inv[i, 1, span] * r1 + inv[i, 2, span] * r2 for i in range(3)
        ]

    for c in range(CHUNKS):
        span = pl.ds(c * rows, rows)
        for side in range(2):

            @pl.when(near[side])
            def _(side=side, c=c):
                for copy in bulk_copies(1 - side, c):
                    copy.wait_recv()

        p, f1, f2 = u[0, span], frac[0, span], frac[1, span]
        q = source[0, span]
        q1, q2 = q * f1, q * f2
        r0 = part[0, span] - (q - q1 - q2)
        r1 = part[1, span] - q1
        r2 = part[2, span] - q2
        for side in range(2):
            h1, h2 = fractions(halo_u[side, 1, span], halo_u[side, 2, span])
            trans = transmissibility(perm[span], halo_k[side, span])
            total = trans * (p - halo_u[side, 0, span])
            s1, s2 = 0.5 * (f1 + h1), 0.5 * (f2 + h2)
            edge[side, 0, span] = trans
            edge[side, 1, span] = 0.5 * total
            edge[side, 2, span] = s1
            edge[side, 3, span] = s2
            flow1, flow2 = total * s1, total * s2
            r0 += total - flow1 - flow2
            r1 += flow1
            r2 += flow2
        res_ref[0, 0, span] = r0
        res_ref[1, 0, span] = r1
        res_ref[2, 0, span] = r2
        save(res_ref, res_hbm, span, c)
        d0, d1, d2 = blocks(span, -r0, -r1, -r2)
        g1, g2 = slope[0, span] * d1, slope[1, span] * d2
        mean = f1 * g1 + f2 * g2
        send_d[0, span] = d0
        send_d[1, span] = f1 * (g1 - mean)
        send_d[2, span] = f2 * (g2 - mean)
        corr[0, span] = d1
        corr[1, span] = d2
        for side in range(2):

            @pl.when(near[side])
            def _(side=side, c=c):
                tangent_copy(side, c).start()

    message_d[...] = jnp.zeros_like(message_d)
    for k in range(caps):
        message_d[k : k + 1, :n] = pick(send_d[0], k)
    inbox_d[me] = message_d[...]

    @pl.loop(1, n)
    def _(step):
        well_copy(message_d, inbox_d, welld_send, welld_recv, step).start()

    dp, df1, df2 = send_d[0], send_d[1], send_d[2]
    q = source[0]
    w1, w2 = q * df1, q * df2
    part[0] = res_ref[0, 0] + accum[0] * dp + (w1 + w2)
    part[1] = res_ref[1, 0] + accum[1] * corr[0] - w1
    part[2] = res_ref[2, 0] + accum[2] * corr[1] - w2
    for axis, size in ((0, ny), (1, nz)):
        total = face[axis, 0] * (dp - pltpu.roll(dp, size - 1, axis))
        flow1 = total * face[axis, 2] + face[axis, 1] * (df1 + pltpu.roll(df1, size - 1, axis))
        flow2 = total * face[axis, 3] + face[axis, 1] * (df2 + pltpu.roll(df2, size - 1, axis))
        flow0 = total - flow1 - flow2
        for i, flow in enumerate((flow0, flow1, flow2)):
            part[i] += flow - pltpu.roll(flow, 1, axis)

    @pl.loop(1, n)
    def _(step):
        well_arrival(message_d, inbox_d, welld_send, welld_recv, step).wait_recv()

    press = [turned(inbox_d[:, k, :n]) for k in range(caps)]
    flows = []
    for k in range(caps):
        lift = sum(jnp.sum(t * b, axis=1, keepdims=True) for t, b in zip(shares[k], press))
        flows.append(my_weight[k] * (lift - own(press[k])))
    source[1] = spread(flows)

    for c in range(CHUNKS):
        span = pl.ds(c * rows, rows)
        for side in range(2):

            @pl.when(near[side])
            def _(side=side, c=c):
                tangent_copy(1 - side, c).wait_recv()

        dp, df1, df2 = send_d[0, span], send_d[1, span], send_d[2, span]
        f1, f2 = frac[0, span], frac[1, span]
        q = source[1, span]
        q1, q2 = q * f1, q * f2
        r0 = part[0, span] - (q - q1 - q2)
        r1 = part[1, span] - q1
        r2 = part[2, span] - q2
        for side in range(2):
            total = edge[side, 0, span] * (dp - halo_d[side, 0, span])
            half = edge[side, 1, span]
            flow1 = total * edge[side, 2, span] + half * (df1 + halo_d[side, 1, span])
            flow2 = total * edge[side, 3, span] + half * (df2 + halo_d[side, 2, span])
            r0 += total - flow1 - flow2
            r1 += flow1
            r2 += flow2
        e0, e1, e2 = blocks(span, -r0, -r1, -r2)
        new_ref[0, 0, span] = u[0, span] + (dp + e0)
        new_ref[1, 0, span] = u[1, span] + (corr[0, span] + e1)
        new_ref[2, 0, span] = u[2, span] + (corr[1, span] + e2)
        save(new_ref, new_hbm, span, CHUNKS + c)

    for copy in saves:
        copy.wait()

    for c in range(CHUNKS):
        for side in range(2):

            @pl.when(near[side])
            def _(side=side, c=c):
                for copy in bulk_copies(side, c):
                    copy.wait_send()
                tangent_copy(side, c).wait_send()

    @pl.loop(1, n)
    def _(step):
        well_copy(message, inbox, well_send, well_recv, step).wait_send()
        well_copy(message_d, inbox_d, welld_send, welld_recv, step).wait_send()


def store(*refs):
    ins, outs, held, load_sem, save_sem = refs[:3], refs[3:6], refs[6:9], refs[9], refs[10]
    loads = [pltpu.make_async_copy(ins[i], held[i], load_sem.at[i]) for i in range(3)]
    saves = [pltpu.make_async_copy(held[i], outs[i], save_sem.at[i]) for i in range(3)]
    for load in loads:
        load.start()
    for load, save in zip(loads, saves):
        load.wait()
        save.start()
    for save in saves:
        save.wait()


def shards(
    state,
    old_state,
    pore_volume,
    permeability,
    inverse_blocks,
    perf_cells,
    perf_wells,
    well_index,
    well_rates,
):
    n = lax.axis_size("gx")
    ny, nz = state.shape[2:]
    caps = perf_cells.shape[0]
    lines = -(-(3 * caps + 1) // 8) * 8
    width = -(-max(n, well_rates.shape[0]) // 128) * 128
    hbm_spec = pl.BlockSpec(memory_space=pltpu.HBM)

    def planes(*lead):
        return pltpu.VMEM((*lead, ny, nz), jnp.float32)

    dma = pltpu.SemaphoreType.DMA
    out_shape = (
        jax.ShapeDtypeStruct(state.shape, jnp.float32),
        jax.ShapeDtypeStruct(state.shape, jnp.float32),
        jax.ShapeDtypeStruct((1, well_rates.shape[0]), jnp.float32),
    )
    results = pl.pallas_call(
        functools.partial(kernel, n),
        out_shape=out_shape,
        in_specs=[hbm_spec] * 9,
        out_specs=(hbm_spec,) * 3,
        scratch_shapes=[
            planes(3, 1),
            planes(3, 1),
            pltpu.VMEM((1, well_rates.shape[0]), jnp.float32),
            dma((2 * CHUNKS + 1,)),
            planes(3),
            planes(3),
            planes(),
            planes(),
            planes(3, 3),
            pltpu.VMEM(perf_cells.shape, jnp.int32),
            pltpu.VMEM(perf_wells.shape, jnp.int32),
            pltpu.VMEM(well_index.shape, jnp.float32),
            pltpu.VMEM((1, well_rates.shape[0]), jnp.float32),
            planes(2, 3),
            planes(2),
            planes(2, 3),
            planes(3),
            planes(2),
            planes(2),
            planes(2),
            planes(3),
            planes(2, 4),
            planes(2, 4),
            planes(3),
            planes(2),
            pltpu.VMEM((lines, width), jnp.float32),
            pltpu.VMEM((n, lines, width), jnp.float32),
            pltpu.VMEM((caps, width), jnp.float32),
            pltpu.VMEM((n, caps, width), jnp.float32),
            dma((9,)),
            dma((n,)),
            dma((n,)),
            dma((n,)),
            dma((n,)),
            dma((2, CHUNKS, 2)),
            dma((2, CHUNKS, 2)),
            dma((2, CHUNKS)),
            dma((2, CHUNKS)),
        ],
        compiler_params=pltpu.CompilerParams(
            collective_id=0, has_side_effects=True, vmem_limit_bytes=VMEM_LIMIT
        ),
    )(
        state,
        old_state,
        pore_volume,
        permeability,
        inverse_blocks,
        perf_cells,
        perf_wells,
        well_index,
        well_rates.reshape(1, -1),
    )
    new_state, residual, bottom = pl.pallas_call(
        store,
        out_shape=out_shape,
        in_specs=[pl.BlockSpec(memory_space=pl.ANY)] * 3,
        out_specs=(hbm_spec,) * 3,
        scratch_shapes=[pltpu.VMEM(shape.shape, shape.dtype) for shape in out_shape]
        + [dma((3,)), dma((3,))],
        compiler_params=pltpu.CompilerParams(vmem_limit_bytes=VMEM_LIMIT),
    )(*results)
    return new_state, residual, bottom.reshape(-1)


def solution(mesh):
    return jax.shard_map(
        shards,
        mesh=mesh,
        in_specs=(
            P(None, ("groups", "gx"), None, None),
            P(None, ("groups", "gx"), None, None),
            P(("groups", "gx"), None, None),
            P(("groups", "gx"), None, None),
            P(None, None, ("groups", "gx"), None, None),
            P(None, ("groups", "gx")),
            P(None, ("groups", "gx")),
            P(None, ("groups", "gx")),
            P(("groups", "gx")),
        ),
        out_specs=(
            P(None, ("groups", "gx"), None, None),
            P(None, ("groups", "gx"), None, None),
            P(("groups", "gx")),
        ),
        check_vma=False,
    )
```

```python
import functools

import jax
import jax.numpy as jnp
from jax import lax
from jax.experimental import pallas as pl
from jax.experimental.pallas import tpu as pltpu
from jax.sharding import PartitionSpec as P

CHUNKS = 4
VMEM_LIMIT = 62 * 1024 * 1024
MESH = pl.DeviceIdType.MESH
EXACT = lax.Precision.HIGHEST


def contract(left, right, left_dim, right_dim):
    return lax.dot_general(
        left,
        right,
        (((left_dim,), (right_dim,)), ((), ())),
        precision=EXACT,
        preferred_element_type=jnp.float32,
    )


def fractions(first, second):
    e1 = jnp.exp(jnp.tanh(first))
    e2 = jnp.exp(jnp.tanh(second))
    inverse = 1.0 / (1.0 + e1 + e2)
    return e1 * inverse, e2 * inverse


def transmissibility(k_a, k_b):
    return 2.0 * k_a * k_b / (k_a + k_b)


def kernel(
    n,
    state_hbm,
    old_hbm,
    pore_hbm,
    perm_hbm,
    inv_hbm,
    cells_hbm,
    wells_hbm,
    index_hbm,
    rates_hbm,
    new_hbm,
    res_hbm,
    bottom_hbm,
    new_ref,
    res_ref,
    bottom_ref,
    save_sem,
    u,
    old,
    pore,
    perm,
    inv,
    cells_ref,
    wells_ref,
    index_ref,
    rates_ref,
    halo_u,
    halo_k,
    halo_d,
    send_d,
    corr,
    frac,
    slope,
    accum,
    face,
    edge,
    part,
    source,
    message,
    inbox,
    message_d,
    inbox_d,
    load_sem,
    well_send,
    well_recv,
    welld_send,
    welld_recv,
    bulk_send,
    bulk_recv,
    bulkd_send,
    bulkd_recv,
):
    me = lax.axis_index("gx")
    ny, nz = perm.shape
    rows = ny // CHUNKS
    caps = cells_ref.shape[0]
    nwell = rates_ref.shape[1]

    loads = [
        pltpu.make_async_copy(state_hbm.at[:, 0], u, load_sem.at[0]),
        pltpu.make_async_copy(perm_hbm.at[0], perm, load_sem.at[1]),
        pltpu.make_async_copy(old_hbm.at[:, 0], old, load_sem.at[2]),
        pltpu.make_async_copy(pore_hbm.at[0], pore, load_sem.at[3]),
        pltpu.make_async_copy(inv_hbm.at[:, :, 0], inv, load_sem.at[4]),
        pltpu.make_async_copy(cells_hbm, cells_ref, load_sem.at[5]),
        pltpu.make_async_copy(wells_hbm, wells_ref, load_sem.at[6]),
        pltpu.make_async_copy(index_hbm, index_ref, load_sem.at[7]),
        pltpu.make_async_copy(rates_hbm, rates_ref, load_sem.at[8]),
    ]
    for load in loads[5:] + loads[:5]:
        load.start()

    saves = [pltpu.make_async_copy(bottom_ref, bottom_hbm, save_sem.at[2 * CHUNKS])]

    def save(source_ref, target_ref, span, slot):
        copy = pltpu.make_async_copy(
            source_ref.at[:, :, span], target_ref.at[:, :, span], save_sem.at[slot]
        )
        copy.start()
        saves.append(copy)

    barrier = pltpu.get_barrier_semaphore()

    @pl.loop(1, n)
    def _(step):
        pl.semaphore_signal(
            barrier, inc=1, device_id={"gx": lax.rem(me + step, n)}, device_id_type=MESH
        )

    for load in loads[5:]:
        load.wait()
    cells = cells_ref[...]
    cell_y = cells // nz
    cell_z = cells - cell_y * nz
    at_y = [
        (lax.broadcasted_iota(jnp.int32, (ny, n), 0) == cell_y[k : k + 1]).astype(jnp.float32)
        for k in range(caps)
    ]
    at_z = [
        (lax.broadcasted_iota(jnp.int32, (nz, n), 0) == cell_z[k : k + 1]).astype(jnp.float32)
        for k in range(caps)
    ]

    def pick(plane, k):
        return jnp.sum(contract(plane, at_z[k], 1, 0) * at_y[k], axis=0, keepdims=True)

    each = message.shape[1] // max(n, nwell)
    stride = message.shape[1] // each

    def seat(piece, size):
        line, first = piece // each, piece % each * stride
        return pl.ds(line, 1), pl.ds(first, size)

    def piece_of(box, piece, size):
        line, first = piece // each, piece % each * stride
        return box[:, line, first : first + size]

    wells = wells_ref[...]
    weights = jnp.where(wells >= 0, index_ref[...], 0.0)
    message[...] = jnp.zeros_like(message)
    for k in range(caps):
        message[seat(caps + k, n)] = weights[k : k + 1]
        message[seat(2 * caps + k, n)] = wells[k : k + 1].astype(jnp.float32)
    message[seat(3 * caps, nwell)] = rates_ref[...]
    loads[0].wait()
    for k in range(caps):
        message[seat(k, n)] = pick(u[0], k)
    inbox[me] = message[...]
    loads[1].wait()

    pl.semaphore_wait(barrier, n - 1)

    def well_copy(source_ref, box, sends, receives, step):
        target = lax.rem(me + step, n)
        return pltpu.make_async_remote_copy(
            src_ref=source_ref,
            dst_ref=box.at[me],
            send_sem=sends.at[target],
            recv_sem=receives.at[me],
            device_id={"gx": target},
            device_id_type=MESH,
        )

    def well_arrival(source_ref, box, sends, receives, step):
        origin = lax.rem(me + step, n)
        return pltpu.make_async_remote_copy(
            src_ref=source_ref,
            dst_ref=box.at[origin],
            send_sem=sends.at[origin],
            recv_sem=receives.at[origin],
            device_id={"gx": origin},
            device_id_type=MESH,
        )

    @pl.loop(1, n)
    def _(step):
        well_copy(message, inbox, well_send, well_recv, step).start()

    near = (me > 0, me < n - 1)
    place = (me - 1, me + 1)

    def bulk_copies(side, c):
        span = pl.ds(c * rows, rows)
        lands = 1 - side
        pairs = (
            (u.at[:, span], halo_u.at[lands, :, span]),
            (perm.at[span], halo_k.at[lands, span]),
        )
        return [
            pltpu.make_async_remote_copy(
                src_ref=src,
                dst_ref=dst,
                send_sem=bulk_send.at[side, c, i],
                recv_sem=bulk_recv.at[lands, c, i],
                device_id={"gx": place[side]},
                device_id_type=MESH,
            )
            for i, (src, dst) in enumerate(pairs)
        ]

    def tangent_copy(side, c):
        span = pl.ds(c * rows, rows)
        lands = 1 - side
        return pltpu.make_async_remote_copy(
            src_ref=send_d.at[:, span],
            dst_ref=halo_d.at[lands, :, span],
            send_sem=bulkd_send.at[side, c],
            recv_sem=bulkd_recv.at[lands, c],
            device_id={"gx": place[side]},
            device_id_type=MESH,
        )

    for c in range(CHUNKS):
        for side in range(2):

            @pl.when(near[side])
            def _(side=side, c=c):
                for copy in bulk_copies(side, c):
                    copy.start()

    for side in range(2):

        @pl.when(jnp.logical_not(near[side]))
        def _(side=side):
            halo_u[side] = jnp.zeros_like(halo_u[side])
            halo_k[side] = jnp.zeros_like(halo_k[side])
            halo_d[side] = jnp.zeros_like(halo_d[side])

    for load in loads[2:4]:
        load.wait()
    p, k_here = u[0], perm[...]
    f1, f2 = fractions(u[1], u[2])
    frac[0] = f1
    frac[1] = f2
    for i in range(3):
        tan = jnp.tanh(u[i])
        rise = 1.0 - tan * tan
        part[i] = pore[...] * (u[i] + 0.5 * tan - (old[i] + 0.5 * jnp.tanh(old[i])))
        accum[i] = pore[...] * (1.0 + 0.5 * rise)
        if i:
            slope[i - 1] = rise

    for axis, size in ((0, ny), (1, nz)):
        last = lax.broadcasted_iota(jnp.int32, (ny, nz), axis) == size - 1
        trans = transmissibility(k_here, pltpu.roll(k_here, size - 1, axis))
        trans = jnp.where(last, 0.0, trans)
        total = trans * (p - pltpu.roll(p, size - 1, axis))
        s1 = 0.5 * (f1 + pltpu.roll(f1, size - 1, axis))
        s2 = 0.5 * (f2 + pltpu.roll(f2, size - 1, axis))
        face[axis, 0] = trans
        face[axis, 1] = 0.5 * total
        face[axis, 2] = s1
        face[axis, 3] = s2
        flow1, flow2 = total * s1, total * s2
        flow0 = total - flow1 - flow2
        for i, flow in enumerate((flow0, flow1, flow2)):
            part[i] += flow - pltpu.roll(flow, 1, axis)

    @pl.loop(1, n)
    def _(step):
        well_arrival(message, inbox, well_send, well_recv, step).wait_recv()

    lane = lax.broadcasted_iota(jnp.int32, (n, n), 1)
    eye = (lax.broadcasted_iota(jnp.int32, (n, n), 0) == lane).astype(jnp.float32)
    mine = lane == me

    def turned(values):
        return contract(eye, values, 1, 1)

    def own(values):
        return jnp.sum(jnp.where(mine, values, 0.0), axis=1, keepdims=True)

    press = [turned(piece_of(inbox, k, n)) for k in range(caps)]
    weight = [piece_of(inbox, caps + k, n) for k in range(caps)]
    well = [piece_of(inbox, 2 * caps + k, n) for k in range(caps)]
    rates = piece_of(inbox, 3 * caps, nwell)
    well_lane = lax.broadcasted_iota(jnp.int32, (n, nwell), 1).astype(jnp.float32)
    my_weight, shares, flows = [], [], []
    for k in range(caps):
        my_well = own(well[k])
        live = my_well >= 0.0
        taken = [jnp.where(well[j] == my_well, weight[j], 0.0) for j in range(caps)]
        whole = sum(jnp.sum(t, axis=1, keepdims=True) for t in taken)
        inverse = 1.0 / jnp.where(live, whole, 1.0)
        rate = jnp.sum(jnp.where(well_lane == my_well, rates, 0.0), axis=1, keepdims=True)
        lift = sum(jnp.sum(t * b, axis=1, keepdims=True) for t, b in zip(taken, press))
        pull = jnp.where(live, own(weight[k]), 0.0)
        flows.append(pull * ((rate + lift) * inverse - own(press[k])))
        my_weight.append(pull)
        shares.append([t * inverse for t in taken])

    def spread(columns):
        plane = None
        for k in range(caps):
            line = jnp.sum(columns[k] * eye, axis=0, keepdims=True)
            term = contract(at_y[k] * line, at_z[k], 1, 1)
            plane = term if plane is None else plane + term
        return plane

    source[0] = spread(flows)

    row_mine = lax.broadcasted_iota(jnp.int32, (n, n), 0) == me
    own_well = lax.broadcasted_iota(jnp.int32, (nwell, n), 0)
    w_sum = jnp.zeros((nwell, 1), jnp.float32)
    p_sum = jnp.zeros((nwell, 1), jnp.float32)
    for k in range(caps):
        line = jnp.sum(jnp.where(row_mine, press[k], 0.0), axis=0, keepdims=True)
        hit = jnp.where(own_well == wells[k : k + 1], weights[k : k + 1], 0.0)
        w_sum += jnp.sum(hit, axis=1, keepdims=True)
        p_sum += jnp.sum(hit * line, axis=1, keepdims=True)
    square = lax.broadcasted_iota(jnp.int32, (nwell, nwell), 0) == lax.broadcasted_iota(
        jnp.int32, (nwell, nwell), 1
    )

    def as_row(column):
        return jnp.sum(jnp.where(square, column, 0.0), axis=0, keepdims=True)

    bottom_ref[...] = (rates_ref[...] + as_row(p_sum)) / as_row(w_sum)
    saves[0].start()

    loads[4].wait()

    def blocks(span, r0, r1, r2):
        return [
            inv[i, 0, span] * r0 + inv[i, 1, span] * r1 + inv[i, 2, span] * r2 for i in range(3)
        ]

    for c in range(CHUNKS):
        span = pl.ds(c * rows, rows)
        for side in range(2):

            @pl.when(near[side])
            def _(side=side, c=c):
                for copy in bulk_copies(1 - side, c):
                    copy.wait_recv()

        p, f1, f2 = u[0, span], frac[0, span], frac[1, span]
        q = source[0, span]
        q1, q2 = q * f1, q * f2
        r0 = part[0, span] - (q - q1 - q2)
        r1 = part[1, span] - q1
        r2 = part[2, span] - q2
        for side in range(2):
            h1, h2 = fractions(halo_u[side, 1, span], halo_u[side, 2, span])
            trans = transmissibility(perm[span], halo_k[side, span])
            total = trans * (p - halo_u[side, 0, span])
            s1, s2 = 0.5 * (f1 + h1), 0.5 * (f2 + h2)
            edge[side, 0, span] = trans
            edge[side, 1, span] = 0.5 * total
            edge[side, 2, span] = s1
            edge[side, 3, span] = s2
            flow1, flow2 = total * s1, total * s2
            r0 += total - flow1 - flow2
            r1 += flow1
            r2 += flow2
        res_ref[0, 0, span] = r0
        res_ref[1, 0, span] = r1
        res_ref[2, 0, span] = r2
        save(res_ref, res_hbm, span, c)
        d0, d1, d2 = blocks(span, -r0, -r1, -r2)
        g1, g2 = slope[0, span] * d1, slope[1, span] * d2
        mean = f1 * g1 + f2 * g2
        send_d[0, span] = d0
        send_d[1, span] = f1 * (g1 - mean)
        send_d[2, span] = f2 * (g2 - mean)
        corr[0, span] = d1
        corr[1, span] = d2
        for side in range(2):

            @pl.when(near[side])
            def _(side=side, c=c):
                tangent_copy(side, c).start()

    message_d[...] = jnp.zeros_like(message_d)
    for k in range(caps):
        message_d[seat(k, n)] = pick(send_d[0], k)
    inbox_d[me] = message_d[...]

    @pl.loop(1, n)
    def _(step):
        well_copy(message_d, inbox_d, welld_send, welld_recv, step).start()

    dp, df1, df2 = send_d[0], send_d[1], send_d[2]
    q = source[0]
    w1, w2 = q * df1, q * df2
    part[0] = res_ref[0, 0] + accum[0] * dp + (w1 + w2)
    part[1] = res_ref[1, 0] + accum[1] * corr[0] - w1
    part[2] = res_ref[2, 0] + accum[2] * corr[1] - w2
    for axis, size in ((0, ny), (1, nz)):
        total = face[axis, 0] * (dp - pltpu.roll(dp, size - 1, axis))
        flow1 = total * face[axis, 2] + face[axis, 1] * (df1 + pltpu.roll(df1, size - 1, axis))
        flow2 = total * face[axis, 3] + face[axis, 1] * (df2 + pltpu.roll(df2, size - 1, axis))
        flow0 = total - flow1 - flow2
        for i, flow in enumerate((flow0, flow1, flow2)):
            part[i] += flow - pltpu.roll(flow, 1, axis)

    @pl.loop(1, n)
    def _(step):
        well_arrival(message_d, inbox_d, welld_send, welld_recv, step).wait_recv()

    press = [turned(piece_of(inbox_d, k, n)) for k in range(caps)]
    flows = []
    for k in range(caps):
        lift = sum(jnp.sum(t * b, axis=1, keepdims=True) for t, b in zip(shares[k], press))
        flows.append(my_weight[k] * (lift - own(press[k])))
    source[1] = spread(flows)

    for c in range(CHUNKS):
        span = pl.ds(c * rows, rows)
        for side in range(2):

            @pl.when(near[side])
            def _(side=side, c=c):
                tangent_copy(1 - side, c).wait_recv()

        dp, df1, df2 = send_d[0, span], send_d[1, span], send_d[2, span]
        f1, f2 = frac[0, span], frac[1, span]
        q = source[1, span]
        q1, q2 = q * f1, q * f2
        r0 = part[0, span] - (q - q1 - q2)
        r1 = part[1, span] - q1
        r2 = part[2, span] - q2
        for side in range(2):
            total = edge[side, 0, span] * (dp - halo_d[side, 0, span])
            half = edge[side, 1, span]
            flow1 = total * edge[side, 2, span] + half * (df1 + halo_d[side, 1, span])
            flow2 = total * edge[side, 3, span] + half * (df2 + halo_d[side, 2, span])
            r0 += total - flow1 - flow2
            r1 += flow1
            r2 += flow2
        e0, e1, e2 = blocks(span, -r0, -r1, -r2)
        new_ref[0, 0, span] = u[0, span] + (dp + e0)
        new_ref[1, 0, span] = u[1, span] + (corr[0, span] + e1)
        new_ref[2, 0, span] = u[2, span] + (corr[1, span] + e2)
        save(new_ref, new_hbm, span, CHUNKS + c)

    for copy in saves:
        copy.wait()

    for c in range(CHUNKS):
        for side in range(2):

            @pl.when(near[side])
            def _(side=side, c=c):
                for copy in bulk_copies(side, c):
                    copy.wait_send()
                tangent_copy(side, c).wait_send()

    @pl.loop(1, n)
    def _(step):
        well_copy(message, inbox, well_send, well_recv, step).wait_send()
        well_copy(message_d, inbox_d, welld_send, welld_recv, step).wait_send()


def store(*refs):
    ins, outs, held, load_sem, save_sem = refs[:3], refs[3:6], refs[6:9], refs[9], refs[10]
    whole = list(zip(ins, outs, held))
    pieces = [whole[2]] + [tuple(ref.at[j] for ref in refs3) for refs3 in whole[:2] for j in range(3)]
    loads = [
        pltpu.make_async_copy(source, hold, load_sem.at[i])
        for i, (source, _, hold) in enumerate(pieces)
    ]
    saves = [
        pltpu.make_async_copy(hold, target, save_sem.at[i])
        for i, (_, target, hold) in enumerate(pieces)
    ]
    for load in loads:
        load.start()
    for load, save in zip(loads, saves):
        load.wait()
        save.start()
    for save in saves:
        save.wait()


def shards(
    state,
    old_state,
    pore_volume,
    permeability,
    inverse_blocks,
    perf_cells,
    perf_wells,
    well_index,
    well_rates,
):
    n = lax.axis_size("gx")
    ny, nz = state.shape[2:]
    caps = perf_cells.shape[0]
    widest = max(n, well_rates.shape[0])
    width = -(-widest // 128) * 128
    each = width // widest
    lines, lines_d = -(-(3 * caps + 1) // each), -(-caps // each)
    hbm_spec = pl.BlockSpec(memory_space=pltpu.HBM)

    def planes(*lead):
        return pltpu.VMEM((*lead, ny, nz), jnp.float32)

    dma = pltpu.SemaphoreType.DMA
    out_shape = (
        jax.ShapeDtypeStruct(state.shape, jnp.float32),
        jax.ShapeDtypeStruct(state.shape, jnp.float32),
        jax.ShapeDtypeStruct((1, well_rates.shape[0]), jnp.float32),
    )
    results = pl.pallas_call(
        functools.partial(kernel, n),
        out_shape=out_shape,
        in_specs=[hbm_spec] * 9,
        out_specs=(hbm_spec,) * 3,
        scratch_shapes=[
            planes(3, 1),
            planes(3, 1),
            pltpu.VMEM((1, well_rates.shape[0]), jnp.float32),
            dma((2 * CHUNKS + 1,)),
            planes(3),
            planes(3),
            planes(),
            planes(),
            planes(3, 3),
            pltpu.VMEM(perf_cells.shape, jnp.int32),
            pltpu.VMEM(perf_wells.shape, jnp.int32),
            pltpu.VMEM(well_index.shape, jnp.float32),
            pltpu.VMEM((1, well_rates.shape[0]), jnp.float32),
            planes(2, 3),
            planes(2),
            planes(2, 3),
            planes(3),
            planes(2),
            planes(2),
            planes(2),
            planes(3),
            planes(2, 4),
            planes(2, 4),
            planes(3),
            planes(2),
            pltpu.VMEM((lines, width), jnp.float32),
            pltpu.VMEM((n, lines, width), jnp.float32),
            pltpu.VMEM((lines_d, width), jnp.float32),
            pltpu.VMEM((n, lines_d, width), jnp.float32),
            dma((9,)),
            dma((n,)),
            dma((n,)),
            dma((n,)),
            dma((n,)),
            dma((2, CHUNKS, 2)),
            dma((2, CHUNKS, 2)),
            dma((2, CHUNKS)),
            dma((2, CHUNKS)),
        ],
        compiler_params=pltpu.CompilerParams(
            collective_id=0, has_side_effects=True, vmem_limit_bytes=VMEM_LIMIT
        ),
    )(
        state,
        old_state,
        pore_volume,
        permeability,
        inverse_blocks,
        perf_cells,
        perf_wells,
        well_index,
        well_rates.reshape(1, -1),
    )
    new_state, residual, bottom = pl.pallas_call(
        store,
        out_shape=out_shape,
        in_specs=[pl.BlockSpec(memory_space=pl.ANY)] * 3,
        out_specs=(hbm_spec,) * 3,
        scratch_shapes=[pltpu.VMEM(shape.shape, shape.dtype) for shape in out_shape]
        + [dma((7,)), dma((7,))],
        compiler_params=pltpu.CompilerParams(vmem_limit_bytes=VMEM_LIMIT),
    )(*results)
    return new_state, residual, bottom.reshape(-1)


def solution(mesh):
    return jax.shard_map(
        shards,
        mesh=mesh,
        in_specs=(
            P(None, ("groups", "gx"), None, None),
            P(None, ("groups", "gx"), None, None),
            P(("groups", "gx"), None, None),
            P(("groups", "gx"), None, None),
            P(None, None, ("groups", "gx"), None, None),
            P(None, ("groups", "gx")),
            P(None, ("groups", "gx")),
            P(None, ("groups", "gx")),
            P(("groups", "gx")),
        ),
        out_specs=(
            P(None, ("groups", "gx"), None, None),
            P(None, ("groups", "gx"), None, None),
            P(("groups", "gx")),
        ),
        check_vma=False,
    )
```

```python
import functools

import jax
import jax.numpy as jnp
from jax import lax
from jax.experimental import pallas as pl
from jax.experimental.pallas import tpu as pltpu
from jax.sharding import PartitionSpec as P

CHUNKS = 4
VMEM_LIMIT = 62 * 1024 * 1024
MESH = pl.DeviceIdType.MESH
EXACT = lax.Precision.HIGHEST


def contract(left, right, left_dim, right_dim):
    return lax.dot_general(
        left,
        right,
        (((left_dim,), (right_dim,)), ((), ())),
        precision=EXACT,
        preferred_element_type=jnp.float32,
    )


def fractions(first, second):
    e1 = jnp.exp(jnp.tanh(first))
    e2 = jnp.exp(jnp.tanh(second))
    inverse = 1.0 / (1.0 + e1 + e2)
    return e1 * inverse, e2 * inverse


def transmissibility(k_a, k_b):
    return 2.0 * k_a * k_b / (k_a + k_b)


def kernel(
    n,
    state_hbm,
    old_hbm,
    pore_hbm,
    perm_hbm,
    inv_hbm,
    cells_hbm,
    wells_hbm,
    index_hbm,
    rates_hbm,
    new_ref,
    res_ref,
    bottom_ref,
    u,
    old,
    pore,
    perm,
    inv,
    cells_ref,
    wells_ref,
    index_ref,
    rates_ref,
    halo_u,
    halo_k,
    halo_d,
    send_d,
    corr,
    frac,
    slope,
    accum,
    face,
    edge,
    part,
    source,
    message,
    inbox,
    message_d,
    inbox_d,
    load_sem,
    well_send,
    well_recv,
    welld_send,
    welld_recv,
    bulk_send,
    bulk_recv,
    bulkd_send,
    bulkd_recv,
):
    me = lax.axis_index("gx")
    ny, nz = perm.shape
    rows = ny // CHUNKS
    caps = cells_ref.shape[0]
    nwell = rates_ref.shape[1]

    loads = [
        pltpu.make_async_copy(state_hbm.at[:, 0], u, load_sem.at[0]),
        pltpu.make_async_copy(perm_hbm.at[0], perm, load_sem.at[1]),
        pltpu.make_async_copy(old_hbm.at[:, 0], old, load_sem.at[2]),
        pltpu.make_async_copy(pore_hbm.at[0], pore, load_sem.at[3]),
        pltpu.make_async_copy(inv_hbm.at[:, :, 0], inv, load_sem.at[4]),
        pltpu.make_async_copy(cells_hbm, cells_ref, load_sem.at[5]),
        pltpu.make_async_copy(wells_hbm, wells_ref, load_sem.at[6]),
        pltpu.make_async_copy(index_hbm, index_ref, load_sem.at[7]),
        pltpu.make_async_copy(rates_hbm, rates_ref, load_sem.at[8]),
    ]
    for load in loads[5:] + loads[:5]:
        load.start()

    barrier = pltpu.get_barrier_semaphore()

    @pl.loop(1, n)
    def _(step):
        pl.semaphore_signal(
            barrier, inc=1, device_id={"gx": lax.rem(me + step, n)}, device_id_type=MESH
        )

    for load in loads[5:]:
        load.wait()
    cells = cells_ref[...]
    cell_y = cells // nz
    cell_z = cells - cell_y * nz
    at_y = [
        (lax.broadcasted_iota(jnp.int32, (ny, n), 0) == cell_y[k : k + 1]).astype(jnp.float32)
        for k in range(caps)
    ]
    at_z = [
        (lax.broadcasted_iota(jnp.int32, (nz, n), 0) == cell_z[k : k + 1]).astype(jnp.float32)
        for k in range(caps)
    ]

    def pick(plane, k):
        return jnp.sum(contract(plane, at_z[k], 1, 0) * at_y[k], axis=0, keepdims=True)

    each = message.shape[1] // max(n, nwell)
    stride = message.shape[1] // each

    def seat(piece, size):
        line, first = piece // each, piece % each * stride
        return pl.ds(line, 1), pl.ds(first, size)

    def piece_of(box, piece, size):
        line, first = piece // each, piece % each * stride
        return box[:, line, first : first + size]

    wells = wells_ref[...]
    weights = jnp.where(wells >= 0, index_ref[...], 0.0)
    message[...] = jnp.zeros_like(message)
    for k in range(caps):
        message[seat(caps + k, n)] = weights[k : k + 1]
        message[seat(2 * caps + k, n)] = wells[k : k + 1].astype(jnp.float32)
    message[seat(3 * caps, nwell)] = rates_ref[...]
    loads[0].wait()
    for k in range(caps):
        message[seat(k, n)] = pick(u[0], k)
    inbox[me] = message[...]
    loads[1].wait()

    pl.semaphore_wait(barrier, n - 1)

    def well_copy(source_ref, box, sends, receives, step):
        target = lax.rem(me + step, n)
        return pltpu.make_async_remote_copy(
            src_ref=source_ref,
            dst_ref=box.at[me],
            send_sem=sends.at[target],
            recv_sem=receives.at[me],
            device_id={"gx": target},
            device_id_type=MESH,
        )

    def well_arrival(source_ref, box, sends, receives, step):
        origin = lax.rem(me + step, n)
        return pltpu.make_async_remote_copy(
            src_ref=source_ref,
            dst_ref=box.at[origin],
            send_sem=sends.at[origin],
            recv_sem=receives.at[origin],
            device_id={"gx": origin},
            device_id_type=MESH,
        )

    @pl.loop(1, n)
    def _(step):
        well_copy(message, inbox, well_send, well_recv, step).start()

    near = (me > 0, me < n - 1)
    place = (me - 1, me + 1)

    def bulk_copies(side, c):
        span = pl.ds(c * rows, rows)
        lands = 1 - side
        pairs = (
            (u.at[:, span], halo_u.at[lands, :, span]),
            (perm.at[span], halo_k.at[lands, span]),
        )
        return [
            pltpu.make_async_remote_copy(
                src_ref=src,
                dst_ref=dst,
                send_sem=bulk_send.at[side, c, i],
                recv_sem=bulk_recv.at[lands, c, i],
                device_id={"gx": place[side]},
                device_id_type=MESH,
            )
            for i, (src, dst) in enumerate(pairs)
        ]

    def tangent_copy(side, c):
        span = pl.ds(c * rows, rows)
        lands = 1 - side
        return pltpu.make_async_remote_copy(
            src_ref=send_d.at[:, span],
            dst_ref=halo_d.at[lands, :, span],
            send_sem=bulkd_send.at[side, c],
            recv_sem=bulkd_recv.at[lands, c],
            device_id={"gx": place[side]},
            device_id_type=MESH,
        )

    for c in range(CHUNKS):
        for side in range(2):

            @pl.when(near[side])
            def _(side=side, c=c):
                for copy in bulk_copies(side, c):
                    copy.start()

    for side in range(2):

        @pl.when(jnp.logical_not(near[side]))
        def _(side=side):
            halo_u[side] = jnp.zeros_like(halo_u[side])
            halo_k[side] = jnp.zeros_like(halo_k[side])
            halo_d[side] = jnp.zeros_like(halo_d[side])

    for load in loads[2:4]:
        load.wait()
    p, k_here = u[0], perm[...]
    f1, f2 = fractions(u[1], u[2])
    frac[0] = f1
    frac[1] = f2
    for i in range(3):
        tan = jnp.tanh(u[i])
        rise = 1.0 - tan * tan
        part[i] = pore[...] * (u[i] + 0.5 * tan - (old[i] + 0.5 * jnp.tanh(old[i])))
        accum[i] = pore[...] * (1.0 + 0.5 * rise)
        if i:
            slope[i - 1] = rise

    for axis, size in ((0, ny), (1, nz)):
        last = lax.broadcasted_iota(jnp.int32, (ny, nz), axis) == size - 1
        trans = transmissibility(k_here, pltpu.roll(k_here, size - 1, axis))
        trans = jnp.where(last, 0.0, trans)
        total = trans * (p - pltpu.roll(p, size - 1, axis))
        s1 = 0.5 * (f1 + pltpu.roll(f1, size - 1, axis))
        s2 = 0.5 * (f2 + pltpu.roll(f2, size - 1, axis))
        face[axis, 0] = trans
        face[axis, 1] = 0.5 * total
        face[axis, 2] = s1
        face[axis, 3] = s2
        flow1, flow2 = total * s1, total * s2
        flow0 = total - flow1 - flow2
        for i, flow in enumerate((flow0, flow1, flow2)):
            part[i] += flow - pltpu.roll(flow, 1, axis)

    @pl.loop(1, n)
    def _(step):
        well_arrival(message, inbox, well_send, well_recv, step).wait_recv()

    lane = lax.broadcasted_iota(jnp.int32, (n, n), 1)
    eye = (lax.broadcasted_iota(jnp.int32, (n, n), 0) == lane).astype(jnp.float32)
    mine = lane == me

    def turned(values):
        return contract(eye, values, 1, 1)

    def own(values):
        return jnp.sum(jnp.where(mine, values, 0.0), axis=1, keepdims=True)

    press = [turned(piece_of(inbox, k, n)) for k in range(caps)]
    weight = [piece_of(inbox, caps + k, n) for k in range(caps)]
    well = [piece_of(inbox, 2 * caps + k, n) for k in range(caps)]
    rates = piece_of(inbox, 3 * caps, nwell)
    well_lane = lax.broadcasted_iota(jnp.int32, (n, nwell), 1).astype(jnp.float32)
    my_weight, shares, flows = [], [], []
    for k in range(caps):
        my_well = own(well[k])
        live = my_well >= 0.0
        taken = [jnp.where(well[j] == my_well, weight[j], 0.0) for j in range(caps)]
        whole = sum(jnp.sum(t, axis=1, keepdims=True) for t in taken)
        inverse = 1.0 / jnp.where(live, whole, 1.0)
        rate = jnp.sum(jnp.where(well_lane == my_well, rates, 0.0), axis=1, keepdims=True)
        lift = sum(jnp.sum(t * b, axis=1, keepdims=True) for t, b in zip(taken, press))
        pull = jnp.where(live, own(weight[k]), 0.0)
        flows.append(pull * ((rate + lift) * inverse - own(press[k])))
        my_weight.append(pull)
        shares.append([t * inverse for t in taken])

    def spread(columns):
        plane = None
        for k in range(caps):
            line = jnp.sum(columns[k] * eye, axis=0, keepdims=True)
            term = contract(at_y[k] * line, at_z[k], 1, 1)
            plane = term if plane is None else plane + term
        return plane

    source[0] = spread(flows)

    row_mine = lax.broadcasted_iota(jnp.int32, (n, n), 0) == me
    own_well = lax.broadcasted_iota(jnp.int32, (nwell, n), 0)
    w_sum = jnp.zeros((nwell, 1), jnp.float32)
    p_sum = jnp.zeros((nwell, 1), jnp.float32)
    for k in range(caps):
        line = jnp.sum(jnp.where(row_mine, press[k], 0.0), axis=0, keepdims=True)
        hit = jnp.where(own_well == wells[k : k + 1], weights[k : k + 1], 0.0)
        w_sum += jnp.sum(hit, axis=1, keepdims=True)
        p_sum += jnp.sum(hit * line, axis=1, keepdims=True)
    square = lax.broadcasted_iota(jnp.int32, (nwell, nwell), 0) == lax.broadcasted_iota(
        jnp.int32, (nwell, nwell), 1
    )

    def as_row(column):
        return jnp.sum(jnp.where(square, column, 0.0), axis=0, keepdims=True)

    bottom_ref[...] = (rates_ref[...] + as_row(p_sum)) / as_row(w_sum)
    loads[4].wait()

    def blocks(span, r0, r1, r2):
        return [
            inv[i, 0, span] * r0 + inv[i, 1, span] * r1 + inv[i, 2, span] * r2 for i in range(3)
        ]

    for c in range(CHUNKS):
        span = pl.ds(c * rows, rows)
        for side in range(2):

            @pl.when(near[side])
            def _(side=side, c=c):
                for copy in bulk_copies(1 - side, c):
                    copy.wait_recv()

        p, f1, f2 = u[0, span], frac[0, span], frac[1, span]
        q = source[0, span]
        q1, q2 = q * f1, q * f2
        r0 = part[0, span] - (q - q1 - q2)
        r1 = part[1, span] - q1
        r2 = part[2, span] - q2
        for side in range(2):
            h1, h2 = fractions(halo_u[side, 1, span], halo_u[side, 2, span])
            trans = transmissibility(perm[span], halo_k[side, span])
            total = trans * (p - halo_u[side, 0, span])
            s1, s2 = 0.5 * (f1 + h1), 0.5 * (f2 + h2)
            edge[side, 0, span] = trans
            edge[side, 1, span] = 0.5 * total
            edge[side, 2, span] = s1
            edge[side, 3, span] = s2
            flow1, flow2 = total * s1, total * s2
            r0 += total - flow1 - flow2
            r1 += flow1
            r2 += flow2
        res_ref[0, 0, span] = r0
        res_ref[1, 0, span] = r1
        res_ref[2, 0, span] = r2
        d0, d1, d2 = blocks(span, -r0, -r1, -r2)
        g1, g2 = slope[0, span] * d1, slope[1, span] * d2
        mean = f1 * g1 + f2 * g2
        send_d[0, span] = d0
        send_d[1, span] = f1 * (g1 - mean)
        send_d[2, span] = f2 * (g2 - mean)
        corr[0, span] = d1
        corr[1, span] = d2
        for side in range(2):

            @pl.when(near[side])
            def _(side=side, c=c):
                tangent_copy(side, c).start()

    message_d[...] = jnp.zeros_like(message_d)
    for k in range(caps):
        message_d[seat(k, n)] = pick(send_d[0], k)
    inbox_d[me] = message_d[...]

    @pl.loop(1, n)
    def _(step):
        well_copy(message_d, inbox_d, welld_send, welld_recv, step).start()

    dp, df1, df2 = send_d[0], send_d[1], send_d[2]
    q = source[0]
    w1, w2 = q * df1, q * df2
    part[0] = res_ref[0, 0] + accum[0] * dp + (w1 + w2)
    part[1] = res_ref[1, 0] + accum[1] * corr[0] - w1
    part[2] = res_ref[2, 0] + accum[2] * corr[1] - w2
    for axis, size in ((0, ny), (1, nz)):
        total = face[axis, 0] * (dp - pltpu.roll(dp, size - 1, axis))
        flow1 = total * face[axis, 2] + face[axis, 1] * (df1 + pltpu.roll(df1, size - 1, axis))
        flow2 = total * face[axis, 3] + face[axis, 1] * (df2 + pltpu.roll(df2, size - 1, axis))
        flow0 = total - flow1 - flow2
        for i, flow in enumerate((flow0, flow1, flow2)):
            part[i] += flow - pltpu.roll(flow, 1, axis)

    @pl.loop(1, n)
    def _(step):
        well_arrival(message_d, inbox_d, welld_send, welld_recv, step).wait_recv()

    press = [turned(piece_of(inbox_d, k, n)) for k in range(caps)]
    flows = []
    for k in range(caps):
        lift = sum(jnp.sum(t * b, axis=1, keepdims=True) for t, b in zip(shares[k], press))
        flows.append(my_weight[k] * (lift - own(press[k])))
    source[1] = spread(flows)

    for c in range(CHUNKS):
        span = pl.ds(c * rows, rows)
        for side in range(2):

            @pl.when(near[side])
            def _(side=side, c=c):
                tangent_copy(1 - side, c).wait_recv()

        dp, df1, df2 = send_d[0, span], send_d[1, span], send_d[2, span]
        f1, f2 = frac[0, span], frac[1, span]
        q = source[1, span]
        q1, q2 = q * f1, q * f2
        r0 = part[0, span] - (q - q1 - q2)
        r1 = part[1, span] - q1
        r2 = part[2, span] - q2
        for side in range(2):
            total = edge[side, 0, span] * (dp - halo_d[side, 0, span])
            half = edge[side, 1, span]
            flow1 = total * edge[side, 2, span] + half * (df1 + halo_d[side, 1, span])
            flow2 = total * edge[side, 3, span] + half * (df2 + halo_d[side, 2, span])
            r0 += total - flow1 - flow2
            r1 += flow1
            r2 += flow2
        e0, e1, e2 = blocks(span, -r0, -r1, -r2)
        new_ref[0, 0, span] = u[0, span] + (dp + e0)
        new_ref[1, 0, span] = u[1, span] + (corr[0, span] + e1)
        new_ref[2, 0, span] = u[2, span] + (corr[1, span] + e2)

    for c in range(CHUNKS):
        for side in range(2):

            @pl.when(near[side])
            def _(side=side, c=c):
                for copy in bulk_copies(side, c):
                    copy.wait_send()
                tangent_copy(side, c).wait_send()

    @pl.loop(1, n)
    def _(step):
        well_copy(message, inbox, well_send, well_recv, step).wait_send()
        well_copy(message_d, inbox_d, welld_send, welld_recv, step).wait_send()


def store(*refs):
    copies = [pltpu.make_async_copy(refs[i], refs[3 + i], refs[6].at[i]) for i in range(3)]
    for copy in copies:
        copy.start()
    for copy in copies:
        copy.wait()


def shards(
    state,
    old_state,
    pore_volume,
    permeability,
    inverse_blocks,
    perf_cells,
    perf_wells,
    well_index,
    well_rates,
):
    n = lax.axis_size("gx")
    ny, nz = state.shape[2:]
    caps = perf_cells.shape[0]
    widest = max(n, well_rates.shape[0])
    width = -(-widest // 128) * 128
    each = width // widest
    lines, lines_d = -(-(3 * caps + 1) // each), -(-caps // each)
    hbm_spec = pl.BlockSpec(memory_space=pltpu.HBM)

    def planes(*lead):
        return pltpu.VMEM((*lead, ny, nz), jnp.float32)

    dma = pltpu.SemaphoreType.DMA
    out_shape = (
        jax.ShapeDtypeStruct(state.shape, jnp.float32),
        jax.ShapeDtypeStruct(state.shape, jnp.float32),
        jax.ShapeDtypeStruct((1, well_rates.shape[0]), jnp.float32),
    )
    results = pl.pallas_call(
        functools.partial(kernel, n),
        out_shape=tuple(pltpu.VMEM(shape.shape, shape.dtype) for shape in out_shape),
        in_specs=[hbm_spec] * 9,
        out_specs=(pl.BlockSpec(memory_space=pltpu.VMEM),) * 3,
        scratch_shapes=[
            planes(3),
            planes(3),
            planes(),
            planes(),
            planes(3, 3),
            pltpu.VMEM(perf_cells.shape, jnp.int32),
            pltpu.VMEM(perf_wells.shape, jnp.int32),
            pltpu.VMEM(well_index.shape, jnp.float32),
            pltpu.VMEM((1, well_rates.shape[0]), jnp.float32),
            planes(2, 3),
            planes(2),
            planes(2, 3),
            planes(3),
            planes(2),
            planes(2),
            planes(2),
            planes(3),
            planes(2, 4),
            planes(2, 4),
            planes(3),
            planes(2),
            pltpu.VMEM((lines, width), jnp.float32),
            pltpu.VMEM((n, lines, width), jnp.float32),
            pltpu.VMEM((lines_d, width), jnp.float32),
            pltpu.VMEM((n, lines_d, width), jnp.float32),
            dma((9,)),
            dma((n,)),
            dma((n,)),
            dma((n,)),
            dma((n,)),
            dma((2, CHUNKS, 2)),
            dma((2, CHUNKS, 2)),
            dma((2, CHUNKS)),
            dma((2, CHUNKS)),
        ],
        compiler_params=pltpu.CompilerParams(
            collective_id=0, has_side_effects=True, vmem_limit_bytes=VMEM_LIMIT
        ),
    )(
        state,
        old_state,
        pore_volume,
        permeability,
        inverse_blocks,
        perf_cells,
        perf_wells,
        well_index,
        well_rates.reshape(1, -1),
    )
    new_state, residual, bottom = pl.pallas_call(
        store,
        out_shape=out_shape,
        in_specs=[pl.BlockSpec(memory_space=pltpu.VMEM)] * 3,
        out_specs=(hbm_spec,) * 3,
        scratch_shapes=[dma((3,))],
        compiler_params=pltpu.CompilerParams(vmem_limit_bytes=16 * 1024 * 1024),
    )(*results)
    return new_state, residual, bottom.reshape(-1)


def solution(mesh):
    return jax.shard_map(
        shards,
        mesh=mesh,
        in_specs=(
            P(None, ("groups", "gx"), None, None),
            P(None, ("groups", "gx"), None, None),
            P(("groups", "gx"), None, None),
            P(("groups", "gx"), None, None),
            P(None, None, ("groups", "gx"), None, None),
            P(None, ("groups", "gx")),
            P(None, ("groups", "gx")),
            P(None, ("groups", "gx")),
            P(("groups", "gx")),
        ),
        out_specs=(
            P(None, ("groups", "gx"), None, None),
            P(None, ("groups", "gx"), None, None),
            P(("groups", "gx")),
        ),
        check_vma=False,
    )
```
